256 devices in a mesh: gx: 8 (over z), gy: 32 (over y, x, core).
Axes of the slice: x: 4, y: 4, z: 8, core: 2. Of those that a mesh axis runs over, the one named last changes fastest.
Arguments:
- tokens: bfloat16 [512, 8192], P('gy', 'gx'), may hold values from -6 to 6
- gate_weight: bfloat16 [8192, 28672], P('gx', 'gy'), may hold values from -0.0625 to 0.0625
- up_weight: bfloat16 [8192, 28672], P('gx', 'gy'), may hold values from -0.0625 to 0.0625
- down_weight: bfloat16 [28672, 8192], P('gy', 'gx'), may hold values from -0.03125 to 0.03125
- out_grad: bfloat16 [512, 8192], P('gy', 'gx'), may hold values from -6 to 6
Outputs:
- input_grad: bfloat16 [512, 8192], P('gy', 'gx')
- gate_grad: bfloat16 [8192, 28672], P('gx', 'gy')
- up_grad: bfloat16 [8192, 28672], P('gx', 'gy')
- down_grad: bfloat16 [28672, 8192], P('gy', 'gx')
- grad_peaks: float32 [2], replicated
The draws below stay inside these ranges and needn't reach their ends.
All inputs are finite; a program needn't handle non-finite values.
Results may differ from the reference program's by a relative error of at most 0.03.
Values may be sent and summed in bfloat16 or wider, within the bound.
A program may use at most 64 MiB of HBM per device.

```python
import jax
import jax.numpy as jnp
from jax import lax

D = 8192
FF = 28672
TOKENS = 512
N_GX = 8


def steps_of(rng, shape, pieces, least, top_value):
    def one(dim, shards_of):
        steps = jax.random.uniform(jax.random.fold_in(jax.random.fold_in(rng, 6), dim), (shards_of,), jnp.float32, least / len(pieces), top_value / len(pieces))
        return jnp.repeat(jnp.exp(steps), shape[dim] // shards_of).reshape((-1,) + (1,) * (len(shape) - dim - 1))

    loudness = one(*pieces[0])
    for cut in pieces[1:]:
        loudness = loudness * one(*cut)
    return loudness


def gaussian(stream_key, shape, deviation, bound, pieces=(), dtype=jnp.bfloat16):
    array = jax.random.normal(stream_key, shape, jnp.float32) * deviation
    if len(pieces) > 0:
        array = steps_of(stream_key, shape, pieces, -0.22, 0.18) * array
    return jnp.clip(array, min=-bound, max=bound).astype(dtype)


def setup_inputs(seed: int = 0) -> dict:
    arg_keys = jax.random.split(jax.random.key(seed), 6)
    return {
        "tokens": gaussian(arg_keys[0], (TOKENS, D), 1.0, 6.0, ((0, 32), (1, 8))),
        "gate_weight": gaussian(arg_keys[1], (D, FF), D ** -0.5, 0.0625, ((0, 8), (1, 32))),
        "up_weight": gaussian(arg_keys[2], (D, FF), D ** -0.5, 0.0625, ((0, 8), (1, 32))),
        "down_weight": gaussian(arg_keys[3], (FF, D), FF ** -0.5, 0.03125, ((0, 32), (1, 8))),
        "out_grad": gaussian(arg_keys[4], (TOKENS, D), 1.0, 6.0, ((0, 32), (1, 8))),
    }


FP8_MAX = 57344.0
HEADROOM = 8.0


def silu_parts(gate):
    sigma = jax.nn.sigmoid(gate)
    return gate * sigma, sigma * (1.0 + gate * (1.0 - sigma))


def block_sum(left, right):
    width = left.shape[1] // N_GX
    total = jnp.zeros((left.shape[0], right.shape[1]), jnp.float32)
    for block in range(N_GX):
        part = jnp.dot(left[:, block * width:(block + 1) * width], right[block * width:(block + 1) * width], preferred_element_type=jnp.float32)
        rounded = lax.optimization_barrier(part.astype(jnp.bfloat16))
        total = total + rounded.astype(jnp.float32)
    return total


def saturate(values, safe_peak):
    scaled = values * (HEADROOM * FP8_MAX / safe_peak)
    return jnp.clip(scaled, -FP8_MAX, FP8_MAX).astype(jnp.bfloat16)


def reference(tokens, gate_weight, up_weight, down_weight, out_grad):
    gate = block_sum(tokens, gate_weight)
    up_val = block_sum(tokens, up_weight)
    act, slope = silu_parts(gate)
    hidden = (act * up_val).astype(jnp.bfloat16)
    hidden_grad = block_sum(out_grad, down_weight.T)
    pre_gate = hidden_grad * up_val * slope
    pre_up = hidden_grad * act
    peak_gate = jnp.max(jnp.abs(pre_gate))
    peak_up = jnp.max(jnp.abs(pre_up))
    safe_gate = peak_gate + 1e-6
    safe_up = peak_up + 1e-6
    coded_gate = saturate(pre_gate, safe_gate)
    coded_up = saturate(pre_up, safe_up)
    back_gate = safe_gate / (HEADROOM * FP8_MAX)
    back_up = safe_up / (HEADROOM * FP8_MAX)
    contract = (((1,), (1,)), ((), ()))
    input_grad = back_gate * lax.dot_general(coded_gate, gate_weight, contract, preferred_element_type=jnp.float32)
    input_grad = input_grad + back_up * lax.dot_general(coded_up, up_weight, contract, preferred_element_type=jnp.float32)
    rows = (((0,), (0,)), ((), ()))
    gate_grad = (back_gate * lax.dot_general(tokens, coded_gate, rows, preferred_element_type=jnp.float32)).astype(jnp.bfloat16)
    up_grad = (back_up * lax.dot_general(tokens, coded_up, rows, preferred_element_type=jnp.float32)).astype(jnp.bfloat16)
    down_grad = lax.dot_general(hidden, out_grad, rows, preferred_element_type=jnp.float32).astype(jnp.bfloat16)
    return input_grad.astype(jnp.bfloat16), gate_grad, up_grad, down_grad, jnp.stack([peak_gate, peak_up])
```

```python
import functools

import jax
import jax.numpy as jnp
from jax import lax
from jax.experimental import pallas as pl
from jax.experimental.pallas import tpu as pltpu
from jax.sharding import PartitionSpec as P

MESH = pl.DeviceIdType.MESH
FP8_MAX = 57344.0
HEADROOM = 8.0
TOP = HEADROOM * FP8_MAX
NZ, NY, NX, ROWS = 8, 4, 4, 16
GROUPS = (0, 1, 3, 2)
GATE, UP, HGRAD = 0, 1, 2
PRE_GATE, HIDDEN, PRE_UP = 0, 1, 2


def dot(a, b):
    return jnp.dot(a, b, preferred_element_type=jnp.float32)


def device(z, y, x, c):
    return (lax.rem(z + NZ, NZ), (lax.rem(y + NY, NY) * NX + lax.rem(x + NX, NX)) * 2 + c)


def main_kernel(
    tok_hbm, grad_hbm, wg_hbm, wu_hbm, wd_hbm,
    ig_ref, peak_ref, tok_out, grad_out, back_out,
    xy, wg, wu, wd, wdt, wgt, wut, part, rs_send, rs_recv, back, coded, ig_part, ig_recv, row_sum, row_recv,
    pk, pk_recv,
    w_sem, x_send, x_recv, f_send, f_recv, y_send, y_recv, g_send, g_recv,
    r_send, r_recv, a_send, a_recv, p_send, p_recv, c_send, c_recv, d_send, d_recv, o_sem,
):
    z, gy = lax.axis_index("gx"), lax.axis_index("gy")
    y, x, c = gy // 8, lax.rem(gy // 2, NX), lax.rem(gy, 2)
    mine = c * NX + x
    partner = device(z, y, x, 1 - c)
    ups = (device(z + 1, y, x, c), device(z - 1, y, x, c))
    sends = []

    def remote(src, dst, s_sem, r_sem, dev):
        return pltpu.make_async_remote_copy(
            src_ref=src, dst_ref=dst, send_sem=s_sem, recv_sem=r_sem, device_id=dev, device_id_type=MESH
        )

    def send(src, dst, s_sem, r_sem, dev):
        copy = remote(src, dst, s_sem, r_sem, dev)
        copy.start()
        sends.append(copy)

    def arrived(ref, s_sem, r_sem):
        remote(ref, ref, s_sem, r_sem, partner).wait_recv()

    def rows(j, n=1):
        return pl.ds(pl.multiple_of(j * ROWS, ROWS), n * ROWS)

    def chunk(k):
        return lax.rem(z + k + 2 * NZ, NZ)

    w_copies = [
        pltpu.make_async_copy(src, dst, w_sem.at[i])
        for i, (src, dst) in enumerate(
            ((tok_hbm, xy.at[0, 0, rows(mine)]), (grad_hbm, xy.at[1, 0, rows(mine)]), (wd_hbm, wd), (wg_hbm, wg), (wu_hbm, wu))
        )
    ]
    for copy in w_copies:
        copy.start()

    barrier = pltpu.get_barrier_semaphore()
    greet = [partner, *ups]
    greet += [device(z, y, x + i, c) for i in (1, 2, 3)] + [device(z, y + i, x, c) for i in (1, 2, 3)]
    for dev in greet:
        pl.semaphore_signal(barrier, inc=1, device_id=dev, device_id_type=MESH)
    w_copies[0].wait()
    w_copies[1].wait()
    pl.semaphore_wait(barrier, len(greet))

    for a in range(2):
        ref = xy.at[a, 0, rows(mine)]
        for i in (1, 3, 2):
            send(ref, ref, x_send.at[a, i - 1], x_recv.at[a, i - 1], device(z, y, x + i, c))
        send(ref, ref, f_send.at[a, 0], f_recv.at[a, 0], partner)

    w_copies[2].wait()
    wdt[...] = wd[...].T

    def row_forward(a):
        for i in (1, 3, 2):
            ref = xy.at[a, 0, rows(c * NX + lax.rem(x - i + NX, NX))]
            arrived(ref, x_send.at[a, i - 1], x_recv.at[a, i - 1])
            send(ref, ref, f_send.at[a, i], f_recv.at[a, i], partner)

    def row_done(a):
        for i in range(4):
            ref = xy.at[a, 0, rows((1 - c) * NX + lax.rem(x - i + NX, NX))]
            arrived(ref, f_send.at[a, i], f_recv.at[a, i])

    half = rows(c * NX, NX)
    other = rows((1 - c) * NX, NX)

    def column_send(a, dists):
        for i in dists:
            send(xy.at[a, 0, half], xy.at[a, 4 - i, half], y_send.at[a, i - 1], y_recv.at[a, i - 1], device(z, y + i, x, c))

    def column_forward(a, dists):
        for i in dists:
            ref = xy.at[a, 4 - i, half]
            arrived(ref, y_send.at[a, i - 1], y_recv.at[a, i - 1])
            send(ref, ref, g_send.at[a, i - 1], g_recv.at[a, i - 1], partner)

    def column_done(a, d):
        arrived(xy.at[a, d, other], g_send.at[a, 3 - d], g_recv.at[a, 3 - d])

    def forward_products(d):
        part[d, GATE] = dot(xy[0, d], wg[...])
        part[d, UP] = dot(xy[0, d], wu[...])

    def grad_products(d):
        part[d, HGRAD] = dot(xy[1, d], wdt[...])

    def span(kind, s, side, d):
        if kind == "gu":
            return (0, 2) if s else ((0, 1), (1, 2))[side]
        return (2, 3) if s or (side == 0) == (d in GROUPS[:2]) else None

    def reduce_step(kind, d, s):
        k = 0 if kind == "gu" else 1
        for side in (0, 1):
            now = span(kind, s, side, d)
            if now is None:
                continue
            j = chunk(4 - s if side == 0 else s - 4)
            before = span(kind, s - 1, side, d) if s else None
            if before is not None:
                lo, hi = before
                arrived(rs_recv.at[side, d, s - 1, lo:hi], r_send.at[side, d, s - 1, k], r_recv.at[side, d, s - 1, k])
            for a in range(*now):
                total = part[d, a, rows(j)]
                if before is not None and before[0] <= a < before[1]:
                    total += rs_recv[side, d, s - 1, a].astype(jnp.float32)
                rs_send[side, d, s, a] = total.astype(jnp.bfloat16)
            lo, hi = now
            send(
                rs_send.at[side, d, s, lo:hi], rs_recv.at[side, d, s, lo:hi],
                r_send.at[side, d, s, k], r_recv.at[side, d, s, k], ups[side],
            )

    def finish(d):
        for side in (0, 1):
            arrived(rs_recv.at[side, d, 3, 0:2], r_send.at[side, d, 3, 0], r_recv.at[side, d, 3, 0])
            arrived(rs_recv.at[side, d, 3, 2:3], r_send.at[side, d, 3, 1], r_recv.at[side, d, 3, 1])
        total = [
            part[d, a, rows(z)] + rs_recv[0, d, 3, a].astype(jnp.float32) + rs_recv[1, d, 3, a].astype(jnp.float32)
            for a in range(3)
        ]
        gate, up_val, hidden_grad = total
        sigma = jax.nn.sigmoid(gate)
        act = gate * sigma
        slope = sigma * (1.0 + gate * (1.0 - sigma))
        pre_gate = hidden_grad * up_val * slope
        pre_up = hidden_grad * act
        back[PRE_GATE, d, rows(z)] = pre_gate.astype(jnp.bfloat16)
        back[HIDDEN, d, rows(z)] = (act * up_val).astype(jnp.bfloat16)
        back[PRE_UP, d, rows(z)] = pre_up.astype(jnp.bfloat16)
        for i, values in enumerate((pre_gate, pre_up)):
            top = jnp.abs(values)
            top = jnp.max(top.reshape(2, 8, top.shape[1]), axis=0)
            best = top[:, 0:128]
            for k in range(1, top.shape[1] // 128):
                best = jnp.maximum(best, top[:, k * 128 : (k + 1) * 128])
            if d != GROUPS[0]:
                best = jnp.maximum(best, pk[0, i * 8 : i * 8 + 8])
            pk[0, i * 8 : i * 8 + 8] = best

    def spread_span(d, t, side):
        if t < 3:
            return 0, 3
        return ((0, 2), (2, 3))[side] if d in GROUPS[:2] else ((0, 1), (1, 3))[side]

    def landed(d, t):
        for side in (0, 1):
            j = chunk(-t - 1 if side == 0 else t + 1)
            lo, hi = spread_span(d, t, side)
            arrived(back.at[lo:hi, d, rows(j)], a_send.at[side, d, t], a_recv.at[side, d, t])

    def spread(d, t):
        if t:
            landed(d, t - 1)
        for side in (0, 1):
            j = chunk(-t if side == 0 else t)
            lo, hi = spread_span(d, t, side)
            ref = back.at[lo:hi, d, rows(j)]
            send(ref, ref, a_send.at[side, d, t], a_recv.at[side, d, t], ups[side])

    row_devs = [device(z, y, x + i % 4, c if i < 4 else 1 - c) for i in range(1, 8)]
    col_devs = [device(z, y + i, x, c) for i in range(1, 4)]
    z_devs = [device(z + i, y, x, c) for i in range(1, 8)]
    stages = ((0, row_devs), (7, col_devs), (10, z_devs))

    def peaks_send(stage):
        first, devs = stages[stage]
        for i, dev in enumerate(devs):
            send(pk.at[stage], pk_recv.at[first + i], p_send.at[first + i], p_recv.at[first + i], dev)

    def peaks_wait(stage):
        first, devs = stages[stage]
        best = pk[stage]
        for i in range(len(devs)):
            arrived(pk_recv.at[first + i], p_send.at[first + i], p_recv.at[first + i])
        for i in range(len(devs)):
            best = jnp.maximum(best, pk_recv[first + i])
        pk[stage + 1] = best

    parts = ((0, 1, -1), (2, -2), (3, -3), (4,))
    starts = (0, 3, 5, 7)

    def input_products(q):
        n = len(parts[q])
        peak_g = jnp.max(pk[3, 0:8]) + 1e-6
        peak_u = jnp.max(pk[3, 8:16]) + 1e-6
        for i, which in enumerate((PRE_GATE, PRE_UP)):
            scale = TOP / (peak_g, peak_u)[i]
            for m, k in enumerate(parts[q]):
                j = chunk(k)
                for d in range(4):
                    values = back[which, d, rows(j)].astype(jnp.float32) * scale
                    row = (d * n + m) * ROWS
                    coded[i, row : row + ROWS] = jnp.clip(values, -FP8_MAX, FP8_MAX).astype(jnp.bfloat16)
        size = 4 * n * ROWS
        first = dot(coded[0, 0:size], wgt[...])
        second = dot(coded[1, 0:size], wut[...])
        total = (peak_g / TOP) * first + (peak_u / TOP) * second
        for d in range(4):
            ig_part[d, starts[q] * ROWS : (starts[q] + n) * ROWS] = total[d * n * ROWS : (d + 1) * n * ROWS].astype(jnp.bfloat16)

    def part_rows(q):
        return slice(starts[q] * ROWS, (starts[q] + len(parts[q])) * ROWS)

    def column_sum_send(q):
        at = part_rows(q)
        for d in (1, 3, 2):
            send(ig_part.at[d, at], ig_recv.at[d, at], c_send.at[q, d - 1], c_recv.at[q, d - 1], device(z, y + d, x, c))

    def row_sum_send(q):
        at = part_rows(q)
        total = ig_part[0, at].astype(jnp.float32)
        for d in (1, 3, 2):
            arrived(ig_recv.at[d, at], c_send.at[q, d - 1], c_recv.at[q, d - 1])
            total += ig_recv[d, at].astype(jnp.float32)
        row_sum[at] = total.astype(jnp.bfloat16)
        for m, k in enumerate(parts[q]):
            j = chunk(k)
            ref = row_sum.at[(starts[q] + m) * ROWS : (starts[q] + m + 1) * ROWS]
            copy = remote(ref, row_recv.at[mine], d_send.at[starts[q] + m], d_recv.at[mine], device(z, y, lax.rem(j, NX), j // NX))

            @pl.when(j != mine)
            def _():
                copy.start()

            @pl.when(j == mine)
            def _():
                row_recv[mine] = ref[...]

    def row_sum_done():
        for q in range(4):
            for m, k in enumerate(parts[q]):
                j = chunk(k)
                ref = row_sum.at[(starts[q] + m) * ROWS : (starts[q] + m + 1) * ROWS]
                copy = remote(ref, row_recv.at[mine], d_send.at[starts[q] + m], d_recv.at[mine], partner)

                @pl.when(j != mine)
                def _():
                    copy.wait_send()

    row_forward(0)
    row_done(0)
    column_send(0, (1, 3))
    w_copies[3].wait()
    w_copies[4].wait()
    forward_products(0)
    reduce_step("gu", 0, 0)
    row_forward(1)
    column_send(1, (1, 3))
    column_send(0, (2,))
    column_send(1, (2,))
    row_done(1)
    grad_products(0)
    reduce_step("gu", 0, 1)
    reduce_step("hg", 0, 0)
    column_forward(0, (1, 3))
    column_done(0, 1)
    forward_products(1)
    reduce_step("gu", 1, 0)
    reduce_step("gu", 0, 2)
    reduce_step("hg", 0, 1)
    column_forward(1, (1, 3))
    column_done(1, 1)
    grad_products(1)
    reduce_step("gu", 1, 1)
    reduce_step("hg", 1, 0)
    column_done(0, 3)
    forward_products(3)
    reduce_step("gu", 3, 0)
    reduce_step("gu", 0, 3)
    reduce_step("hg", 0, 2)
    column_forward(0, (2,))
    column_done(1, 3)
    grad_products(3)
    reduce_step("gu", 1, 2)
    reduce_step("hg", 1, 1)
    reduce_step("gu", 3, 1)
    reduce_step("hg", 3, 0)
    column_done(0, 2)
    forward_products(2)
    reduce_step("gu", 2, 0)
    column_forward(1, (2,))
    reduce_step("hg", 0, 3)
    reduce_step("gu", 1, 3)
    column_done(1, 2)
    grad_products(2)
    reduce_step("hg", 1, 2)
    reduce_step("gu", 3, 2)
    reduce_step("hg", 3, 1)
    reduce_step("gu", 2, 1)
    reduce_step("hg", 2, 0)
    outs = [pltpu.make_async_copy(xy.at[0], tok_out, o_sem.at[0]), pltpu.make_async_copy(xy.at[1], grad_out, o_sem.at[1])]
    for copy in outs:
        copy.start()
    wgt[...] = wg[...].T
    reduce_step("hg", 1, 3)
    reduce_step("gu", 3, 3)
    reduce_step("hg", 3, 2)
    reduce_step("gu", 2, 2)
    reduce_step("hg", 2, 1)
    finish(0)
    spread(0, 0)
    wut[...] = wu[...].T
    reduce_step("hg", 3, 3)
    reduce_step("gu", 2, 3)
    reduce_step("hg", 2, 2)
    finish(1)
    spread(1, 0)
    reduce_step("hg", 2, 3)
    finish(3)
    spread(3, 0)
    spread(0, 1)
    finish(2)
    peaks_send(0)
    spread(2, 0)
    spread(1, 1)
    peaks_wait(0)
    peaks_send(1)
    spread(3, 1)
    peaks_wait(1)
    peaks_send(2)
    spread(2, 1)
    spread(0, 2)
    spread(1, 2)
    peaks_wait(2)
    input_products(0)
    column_sum_send(0)
    spread(3, 2)
    spread(2, 2)
    row_sum_send(0)
    input_products(1)
    column_sum_send(1)
    for d in GROUPS:
        spread(d, 3)
    input_products(2)
    column_sum_send(2)
    row_sum_send(1)
    for d in GROUPS:
        landed(d, 3)
    input_products(3)
    column_sum_send(3)
    copy = pltpu.make_async_copy(back, back_out, o_sem.at[2])
    copy.start()
    outs.append(copy)
    row_sum_send(2)
    row_sum_send(3)
    peak_ref[0] = jnp.max(pk[3, 0:8])
    peak_ref[1] = jnp.max(pk[3, 8:16])
    for i in range(1, 8):
        src = lax.rem(mine + i, 8)
        arrived(row_recv.at[src], d_send.at[0], d_recv.at[src])
    total = row_recv[0].astype(jnp.float32)
    for i in range(1, 8):
        total += row_recv[i].astype(jnp.float32)
    ig_ref[...] = total.astype(jnp.bfloat16)
    row_sum_done()
    for copy in outs:
        copy.wait()
    for copy in sends:
        copy.wait_send()


def weight_kernel(peak_ref, tok_ref, grad_ref, back_ref, gate_ref, up_ref, down_ref, coded):
    tokens = tok_ref.shape[0]
    peak_g, peak_u = peak_ref[0] + 1e-6, peak_ref[1] + 1e-6

    @pl.when(pl.program_id(0) == 0)
    def _():
        for i, (which, peak) in enumerate(((PRE_GATE, peak_g), (PRE_UP, peak_u))):
            values = back_ref[which].astype(jnp.float32) * (TOP / peak)
            coded[i] = jnp.clip(values, -FP8_MAX, FP8_MAX).astype(jnp.bfloat16)

    rows = (((0,), (0,)), ((), ()))
    tok = tok_ref[...]
    for i, (ref, peak) in enumerate(((gate_ref, peak_g), (up_ref, peak_u))):
        ref[...] = ((peak / TOP) * lax.dot_general(tok, coded[i], rows, preferred_element_type=jnp.float32)).astype(jnp.bfloat16)
    down_ref[...] = lax.dot_general(back_ref[HIDDEN], grad_ref[...], rows, preferred_element_type=jnp.float32).astype(jnp.bfloat16)


def local(tokens, gate_weight, up_weight, down_weight, out_grad):
    bf16, f32 = jnp.bfloat16, jnp.float32
    width, hid = gate_weight.shape
    total = NY * 2 * NX * ROWS
    anywhere = pl.BlockSpec(memory_space=pl.ANY)
    vmem, dma = pltpu.VMEM, pltpu.SemaphoreType.DMA
    group = 2 * NX * ROWS
    input_grad, peaks, tok_all, grad_all, back = pl.pallas_call(
        main_kernel,
        name="slab",
        out_shape=(
            jax.ShapeDtypeStruct((ROWS, width), bf16),
            jax.ShapeDtypeStruct((2,), f32),
            jax.ShapeDtypeStruct((NY, group, width), bf16),
            jax.ShapeDtypeStruct((NY, group, width), bf16),
            jax.ShapeDtypeStruct((3, NY, group, hid), bf16),
        ),
        in_specs=[anywhere] * 5,
        out_specs=(
            pl.BlockSpec(memory_space=pltpu.VMEM),
            pl.BlockSpec(memory_space=pltpu.SMEM),
            anywhere,
            anywhere,
            anywhere,
        ),
        scratch_shapes=[
            vmem((2, NY, group, width), bf16),
            vmem((width, hid), bf16),
            vmem((width, hid), bf16),
            vmem((hid, width), bf16),
            vmem((width, hid), bf16),
            vmem((hid, width), bf16),
            vmem((hid, width), bf16),
            vmem((NY, 3, group, hid), f32),
            vmem((2, NY, 4, 3, ROWS, hid), bf16),
            vmem((2, NY, 4, 3, ROWS, hid), bf16),
            vmem((3, NY, group, hid), bf16),
            vmem((2, 3 * NY * ROWS, hid), bf16),
            vmem((NY, NZ * ROWS, width), bf16),
            vmem((NY, NZ * ROWS, width), bf16),
            vmem((NZ * ROWS, width), bf16),
            vmem((8, ROWS, width), bf16),
            vmem((4, 16, 128), f32),
            vmem((17, 16, 128), f32),
            dma((5,)),
            dma((2, 3)), dma((2, 3)), dma((2, 4)), dma((2, 4)), dma((2, 3)), dma((2, 3)), dma((2, 3)), dma((2, 3)),
            dma((2, NY, 4, 2)), dma((2, NY, 4, 2)), dma((2, NY, 4)), dma((2, NY, 4)), dma((17,)), dma((17,)),
            dma((4, 3)), dma((4, 3)), dma((8,)), dma((8,)), dma((3,)),
        ],
        compiler_params=pltpu.CompilerParams(collective_id=0, has_side_effects=True, vmem_limit_bytes=56 * 2**20),
    )(tokens, out_grad, gate_weight, up_weight, down_weight)
    tile = width // 4
    gate_grad, up_grad, down_grad = pl.pallas_call(
        weight_kernel,
        name="weight_grads",
        grid=(4,),
        out_shape=(
            jax.ShapeDtypeStruct((width, hid), bf16),
            jax.ShapeDtypeStruct((width, hid), bf16),
            jax.ShapeDtypeStruct((hid, width), bf16),
        ),
        in_specs=[
            pl.BlockSpec(memory_space=pltpu.SMEM),
            pl.BlockSpec((total, tile), lambda i: (0, i)),
            pl.BlockSpec((total, tile), lambda i: (0, i)),
            pl.BlockSpec((3, total, hid), lambda i: (0, 0, 0)),
        ],
        out_specs=(
            pl.BlockSpec((tile, hid), lambda i: (i, 0)),
            pl.BlockSpec((tile, hid), lambda i: (i, 0)),
            pl.BlockSpec((hid, tile), lambda i: (0, i)),
        ),
        scratch_shapes=[vmem((2, total, hid), bf16)],
        compiler_params=pltpu.CompilerParams(vmem_limit_bytes=48 * 2**20),
    )(peaks, tok_all.reshape(total, width), grad_all.reshape(total, width), back.reshape(3, total, hid))
    return input_grad, gate_grad, up_grad, down_grad, peaks


def solution(mesh):
    in_specs = (P("gy", "gx"), P("gx", "gy"), P("gx", "gy"), P("gy", "gx"), P("gy", "gx"))
    out_specs = (P("gy", "gx"), P("gx", "gy"), P("gx", "gy"), P("gy", "gx"), P())
    return jax.shard_map(local, mesh=mesh, in_specs=in_specs, out_specs=out_specs, check_vma=False)
```

```python
import functools

import jax
import jax.numpy as jnp
from jax import lax
from jax.experimental import pallas as pl
from jax.experimental.pallas import tpu as pltpu
from jax.sharding import PartitionSpec as P

MESH = pl.DeviceIdType.MESH
FP8_MAX = 57344.0
HEADROOM = 8.0
TOP = HEADROOM * FP8_MAX
NZ, NY, NX, ROWS = 8, 4, 4, 16
GROUPS = (0, 1, 3, 2)
GATE, UP, HGRAD = 0, 1, 2
PRE_GATE, PRE_UP, HIDDEN = 0, 1, 2


def dot(a, b):
    return jnp.dot(a, b, preferred_element_type=jnp.float32)


def dot_rows(a, b):
    return lax.dot_general(a, b, (((0,), (0,)), ((), ())), preferred_element_type=jnp.float32)


def device(z, y, x, c):
    return (lax.rem(z + NZ, NZ), (lax.rem(y + NY, NY) * NX + lax.rem(x + NX, NX)) * 2 + c)


def main_kernel(
    tok_hbm, grad_hbm, wg_hbm, wu_hbm, wd_hbm,
    ig_ref, peak_ref, gate_out, up_out, hidden_out, grad_out,
    xy, wg, wu, wd, wdt, wgt, wut, part, rs_send, rs_recv, back, coded, w_grad, ig_part, ig_recv, row_sum, row_recv,
    pk, pk_recv,
    w_sem, x_send, x_recv, f_send, f_recv, y_send, y_recv, g_send, g_recv,
    r_send, r_recv, a_send, a_recv, h_send, h_recv, p_send, p_recv, c_send, c_recv, d_send, d_recv, o_sem,
):
    z, gy = lax.axis_index("gx"), lax.axis_index("gy")
    y, x, c = gy // 8, lax.rem(gy // 2, NX), lax.rem(gy, 2)
    mine = c * NX + x
    partner = device(z, y, x, 1 - c)
    ups = (device(z + 1, y, x, c), device(z - 1, y, x, c))
    sends, outs = [], []

    def remote(src, dst, s_sem, r_sem, dev):
        return pltpu.make_async_remote_copy(
            src_ref=src, dst_ref=dst, send_sem=s_sem, recv_sem=r_sem, device_id=dev, device_id_type=MESH
        )

    def send(src, dst, s_sem, r_sem, dev):
        copy = remote(src, dst, s_sem, r_sem, dev)
        copy.start()
        sends.append(copy)

    def arrived(ref, s_sem, r_sem):
        remote(ref, ref, s_sem, r_sem, partner).wait_recv()

    def rows(j, n=1):
        return pl.ds(pl.multiple_of(j * ROWS, ROWS), n * ROWS)

    def of(d, n=1):
        return slice(d * ROWS, (d + n) * ROWS)

    def chunk(k):
        return lax.rem(z + k + 2 * NZ, NZ)

    w_copies = [
        pltpu.make_async_copy(src, dst, w_sem.at[i])
        for i, (src, dst) in enumerate(
            ((tok_hbm, xy.at[0, mine, of(0)]), (grad_hbm, xy.at[1, mine, of(0)]), (wd_hbm, wd), (wg_hbm, wg), (wu_hbm, wu))
        )
    ]
    for copy in w_copies:
        copy.start()

    barrier = pltpu.get_barrier_semaphore()
    greet = [partner, *ups]
    greet += [device(z, y, x + i, c) for i in (1, 2, 3)] + [device(z, y + i, x, c) for i in (1, 2, 3)]
    for dev in greet:
        pl.semaphore_signal(barrier, inc=1, device_id=dev, device_id_type=MESH)
    w_copies[0].wait()
    w_copies[1].wait()
    pl.semaphore_wait(barrier, len(greet))

    def row_send(a):
        ref = xy.at[a, mine, of(0)]
        for i in (1, 3, 2):
            send(ref, ref, x_send.at[a, i - 1], x_recv.at[a, i - 1], device(z, y, x + i, c))
        send(ref, ref, f_send.at[a, 0], f_recv.at[a, 0], partner)

    def column_send(a, piece, dists):
        j = c * NX + lax.rem(x - piece + NX, NX)
        for i in dists:
            send(
                xy.at[a, j, of(0)], xy.at[a, j, of(4 - i)], y_send.at[a, i - 1, piece], y_recv.at[a, i - 1, piece],
                device(z, y + i, x, c),
            )

    def row_forward(a):
        for i in (1, 3, 2):
            ref = xy.at[a, c * NX + lax.rem(x - i + NX, NX), of(0)]
            arrived(ref, x_send.at[a, i - 1], x_recv.at[a, i - 1])
            send(ref, ref, f_send.at[a, i], f_recv.at[a, i], partner)
            column_send(a, i, (1, 3))

    def row_done(a):
        for i in range(4):
            ref = xy.at[a, (1 - c) * NX + lax.rem(x - i + NX, NX), of(0)]
            arrived(ref, f_send.at[a, i], f_recv.at[a, i])

    def half(a, d, core):
        return xy.at[a, pl.ds(core * NX, NX), of(d)]

    def column_forward(a, dists):
        for i in dists:
            for piece in (0, 1, 3, 2):
                ref = xy.at[a, c * NX + lax.rem(x - piece + NX, NX), of(4 - i)]
                arrived(ref, y_send.at[a, i - 1, piece], y_recv.at[a, i - 1, piece])
            ref = half(a, 4 - i, c)
            send(ref, ref, g_send.at[a, i - 1], g_recv.at[a, i - 1], partner)

    def column_done(a, d):
        arrived(half(a, d, 1 - c), g_send.at[a, 3 - d], g_recv.at[a, 3 - d])

    def group(a, d):
        return xy[a, :, of(d)].reshape(2 * NX * ROWS, xy.shape[3])

    def forward_products(d):
        part[d, GATE] = dot(group(0, d), wg[...])
        part[d, UP] = dot(group(0, d), wu[...])

    def grad_products(d):
        part[d, HGRAD] = dot(group(1, d), wdt[...])

    def span(kind, s, side, d):
        if kind == "gu":
            return (0, 2) if s else ((0, 1), (1, 2))[side]
        return (2, 3) if s or (side == 0) == (d in GROUPS[:2]) else None

    def reduce_step(kind, d, s):
        k = 0 if kind == "gu" else 1
        for side in (0, 1):
            now = span(kind, s, side, d)
            if now is None:
                continue
            j = chunk(4 - s if side == 0 else s - 4)
            before = span(kind, s - 1, side, d) if s else None
            if before is not None:
                lo, hi = before
                arrived(rs_recv.at[side, d, s - 1, lo:hi], r_send.at[side, d, s - 1, k], r_recv.at[side, d, s - 1, k])
            for a in range(*now):
                total = part[d, a, rows(j)]
                if before is not None and before[0] <= a < before[1]:
                    total += rs_recv[side, d, s - 1, a].astype(jnp.float32)
                rs_send[side, d, s, a] = total.astype(jnp.bfloat16)
            lo, hi = now
            send(
                rs_send.at[side, d, s, lo:hi], rs_recv.at[side, d, s, lo:hi],
                r_send.at[side, d, s, k], r_recv.at[side, d, s, k], ups[side],
            )

    def finish(d):
        for side in (0, 1):
            arrived(rs_recv.at[side, d, 3, 0:2], r_send.at[side, d, 3, 0], r_recv.at[side, d, 3, 0])
            arrived(rs_recv.at[side, d, 3, 2:3], r_send.at[side, d, 3, 1], r_recv.at[side, d, 3, 1])
        total = [
            part[d, a, rows(z)] + rs_recv[0, d, 3, a].astype(jnp.float32) + rs_recv[1, d, 3, a].astype(jnp.float32)
            for a in range(3)
        ]
        gate, up_val, hidden_grad = total
        sigma = jax.nn.sigmoid(gate)
        act = gate * sigma
        slope = sigma * (1.0 + gate * (1.0 - sigma))
        pre_gate = hidden_grad * up_val * slope
        pre_up = hidden_grad * act
        back[PRE_GATE, z, of(d)] = pre_gate.astype(jnp.bfloat16)
        back[PRE_UP, z, of(d)] = pre_up.astype(jnp.bfloat16)
        back[HIDDEN, z, of(d)] = (act * up_val).astype(jnp.bfloat16)
        for i, values in enumerate((pre_gate, pre_up)):
            top = jnp.abs(values)
            top = jnp.max(top.reshape(2, 8, top.shape[1]), axis=0)
            best = top[:, 0:128]
            for k in range(1, top.shape[1] // 128):
                best = jnp.maximum(best, top[:, k * 128 : (k + 1) * 128])
            if d != GROUPS[0]:
                best = jnp.maximum(best, pk[0, i * 8 : i * 8 + 8])
            pk[0, i * 8 : i * 8 + 8] = best

    def spread_ref(d, t, side):
        j = chunk(-t if side == 0 else t)
        lo, hi = (0, 2) if t < 3 else (side, side + 1)
        return back.at[lo:hi, j, of(d)]

    def landed(d, t):
        for side in (0, 1):
            j = chunk(-t - 1 if side == 0 else t + 1)
            lo, hi = (0, 2) if t < 3 else (side, side + 1)
            arrived(back.at[lo:hi, j, of(d)], a_send.at[side, d, t], a_recv.at[side, d, t])

    def spread(d, t):
        if t:
            landed(d, t - 1)
        for side in (0, 1):
            ref = spread_ref(d, t, side)
            send(ref, ref, a_send.at[side, d, t], a_recv.at[side, d, t], ups[side])

    def hidden_landed(part_of, t):
        for side in (0, 1):
            if t == 3 and side != part_of:
                continue
            j = chunk(-t - 1 if side == 0 else t + 1)
            arrived(back.at[HIDDEN, j, of(2 * part_of, 2)], h_send.at[side, part_of, t], h_recv.at[side, part_of, t])

    def hidden_spread(part_of, t):
        if t:
            hidden_landed(part_of, t - 1)
        for side in (0, 1):
            if t == 3 and side != part_of:
                continue
            ref = back.at[HIDDEN, chunk(-t if side == 0 else t), of(2 * part_of, 2)]
            send(ref, ref, h_send.at[side, part_of, t], h_recv.at[side, part_of, t], ups[side])

    row_devs = [device(z, y, x + i % 4, c if i < 4 else 1 - c) for i in range(1, 8)]
    col_devs = [device(z, y + i, x, c) for i in range(1, 4)]
    z_devs = [device(z + i, y, x, c) for i in range(1, 8)]
    stages = ((0, row_devs), (7, col_devs), (10, z_devs))

    def peaks_send(stage):
        first, devs = stages[stage]
        for i, dev in enumerate(devs):
            send(pk.at[stage], pk_recv.at[first + i], p_send.at[first + i], p_recv.at[first + i], dev)

    def peaks_wait(stage):
        first, devs = stages[stage]
        best = pk[stage]
        for i in range(len(devs)):
            arrived(pk_recv.at[first + i], p_send.at[first + i], p_recv.at[first + i])
        for i in range(len(devs)):
            best = jnp.maximum(best, pk_recv[first + i])
        pk[stage + 1] = best

    def safe_peaks():
        return jnp.max(pk[3, 0:8]) + 1e-6, jnp.max(pk[3, 8:16]) + 1e-6

    parts = ((0, 1, -1), (2, -2), (3, -3), (4,))
    starts = (0, 3, 5, 7)

    def input_products(q):
        peaks = safe_peaks()
        size = 4 * ROWS
        for i, which in enumerate((PRE_GATE, PRE_UP)):
            scale = TOP / peaks[i]
            for k in parts[q]:
                j = chunk(k)
                values = back[which, j].astype(jnp.float32) * scale
                coded[i, j] = jnp.clip(values, -FP8_MAX, FP8_MAX).astype(jnp.bfloat16)
        first, second = (
            dot(jnp.concatenate([coded[i, chunk(k)] for k in parts[q]], axis=0), w[...]) for i, w in enumerate((wgt, wut))
        )
        total = ((peaks[0] / TOP) * first + (peaks[1] / TOP) * second).astype(jnp.bfloat16)
        for m in range(len(parts[q])):
            for d in range(4):
                ig_part[d, of(starts[q] + m)] = total[m * size + d * ROWS : m * size + (d + 1) * ROWS]

    def column_sum_send(q):
        at = of(starts[q], len(parts[q]))
        for d in (1, 3, 2):
            send(ig_part.at[d, at], ig_recv.at[d, at], c_send.at[q, d - 1], c_recv.at[q, d - 1], device(z, y + d, x, c))

    def row_copy(q, m):
        j = chunk(parts[q][m])
        ref = row_sum.at[of(starts[q] + m)]
        k = starts[q] + m
        return j, ref, remote(ref, row_recv.at[mine], d_send.at[k], d_recv.at[mine], device(z, y, lax.rem(j, NX), j // NX))

    def row_sum_send(q):
        at = of(starts[q], len(parts[q]))
        total = ig_part[0, at].astype(jnp.float32)
        for d in (1, 3, 2):
            arrived(ig_recv.at[d, at], c_send.at[q, d - 1], c_recv.at[q, d - 1])
            total += ig_recv[d, at].astype(jnp.float32)
        row_sum[at] = total.astype(jnp.bfloat16)
        for m in range(len(parts[q])):
            j, ref, copy = row_copy(q, m)

            @pl.when(j != mine)
            def _():
                copy.start()

            @pl.when(j == mine)
            def _():
                row_recv[mine] = ref[...]

    def row_sum_finish():
        for i in range(1, 8):
            src = lax.rem(mine + i, 8)
            arrived(row_recv.at[src], d_send.at[0], d_recv.at[src])
        total = row_recv[0].astype(jnp.float32)
        for i in range(1, 8):
            total += row_recv[i].astype(jnp.float32)
        ig_ref[...] = total.astype(jnp.bfloat16)

    def row_sum_sent():
        for q in range(4):
            for m in range(len(parts[q])):
                j, _, copy = row_copy(q, m)

                @pl.when(j != mine)
                def _():
                    copy.wait_send()

    def weight_products(i):
        scale = safe_peaks()[i] / TOP
        width = xy.shape[3]
        total = 2 * NX * 4 * ROWS
        right = coded[i].reshape(total, coded.shape[3])
        for k in range(0, width, 256):
            left = xy[0, :, :, k : k + 256].reshape(total, 256)
            w_grad[i, k : k + 256] = (scale * dot_rows(left, right)).astype(jnp.bfloat16)
        copy = pltpu.make_async_copy(w_grad.at[i], (gate_out, up_out)[i], o_sem.at[i])
        copy.start()
        outs.append(copy)

    def out(src, dst, sem):
        copy = pltpu.make_async_copy(src, dst, o_sem.at[sem])
        copy.start()
        outs.append(copy)

    row_send(0)
    column_send(0, 0, (1, 3))
    row_send(1)
    w_copies[2].wait()
    wdt[...] = wd[...].T
    row_forward(0)
    row_done(0)
    w_copies[3].wait()
    w_copies[4].wait()
    forward_products(0)
    reduce_step("gu", 0, 0)
    column_send(1, 0, (1, 3))
    row_forward(1)
    for piece in range(4):
        column_send(0, piece, (2,))
    for piece in range(4):
        column_send(1, piece, (2,))
    row_done(1)
    grad_products(0)
    reduce_step("hg", 0, 0)
    column_forward(0, (3, 1))
    reduce_step("gu", 0, 1)
    column_done(0, 1)
    forward_products(1)
    reduce_step("gu", 1, 0)
    reduce_step("hg", 0, 1)
    reduce_step("gu", 0, 2)
    column_forward(1, (3, 1))
    column_done(1, 1)
    grad_products(1)
    reduce_step("hg", 1, 0)
    reduce_step("gu", 1, 1)
    reduce_step("hg", 0, 2)
    column_done(0, 3)
    forward_products(3)
    reduce_step("gu", 3, 0)
    reduce_step("gu", 0, 3)
    column_done(1, 3)
    grad_products(3)
    reduce_step("hg", 3, 0)
    reduce_step("gu", 1, 2)
    reduce_step("hg", 1, 1)
    column_forward(0, (2,))
    reduce_step("gu", 3, 1)
    reduce_step("hg", 0, 3)
    column_done(0, 2)
    forward_products(2)
    reduce_step("gu", 2, 0)
    column_forward(1, (2,))
    reduce_step("gu", 1, 3)
    reduce_step("hg", 1, 2)
    reduce_step("gu", 3, 2)
    reduce_step("hg", 3, 1)
    column_done(1, 2)
    grad_products(2)
    reduce_step("hg", 2, 0)
    reduce_step("gu", 2, 1)
    out(xy.at[1], grad_out, 3)
    reduce_step("hg", 1, 3)
    reduce_step("gu", 3, 3)
    reduce_step("hg", 3, 2)
    reduce_step("gu", 2, 2)
    reduce_step("hg", 2, 1)
    finish(0)
    spread(0, 0)
    reduce_step("hg", 3, 3)
    reduce_step("gu", 2, 3)
    reduce_step("hg", 2, 2)
    finish(1)
    spread(1, 0)
    reduce_step("hg", 2, 3)
    finish(3)
    spread(3, 0)
    spread(0, 1)
    wgt[...] = wg[...].T
    finish(2)
    peaks_send(0)
    spread(2, 0)
    spread(1, 1)
    wut[...] = wu[...].T
    peaks_wait(0)
    peaks_send(1)
    spread(3, 1)
    spread(0, 2)
    peaks_wait(1)
    peaks_send(2)
    spread(2, 1)
    spread(1, 2)
    hidden_spread(0, 0)
    hidden_spread(1, 0)
    spread(3, 2)
    spread(2, 2)
    peaks_wait(2)
    input_products(0)
    column_sum_send(0)
    spread(0, 3)
    spread(1, 3)
    input_products(1)
    column_sum_send(1)
    spread(3, 3)
    spread(2, 3)
    hidden_spread(0, 1)
    hidden_spread(1, 1)
    row_sum_send(0)
    input_products(2)
    column_sum_send(2)
    row_sum_send(1)
    for d in GROUPS:
        landed(d, 3)
    input_products(3)
    column_sum_send(3)
    hidden_spread(0, 2)
    hidden_spread(1, 2)
    row_sum_send(2)
    weight_products(0)
    row_sum_send(3)
    hidden_spread(0, 3)
    hidden_spread(1, 3)
    weight_products(1)
    row_sum_finish()
    peak_ref[0] = jnp.max(pk[3, 0:8])
    peak_ref[1] = jnp.max(pk[3, 8:16])
    hidden_landed(0, 3)
    hidden_landed(1, 3)
    out(back.at[HIDDEN], hidden_out, 2)
    row_sum_sent()
    for copy in outs:
        copy.wait()
    for copy in sends:
        copy.wait_send()


def weight_kernel(gate_in, up_in, hidden, out_grad, ig_in, peak_in, gate_ref, up_ref, down_ref, ig_ref, peak_ref, down, sem):
    copies = [pltpu.make_async_copy(gate_in, gate_ref, sem.at[0]), pltpu.make_async_copy(up_in, up_ref, sem.at[1])]
    for copy in copies:
        copy.start()
    for k in range(0, down.shape[0], 256):
        at = slice(k, min(k + 256, down.shape[0]))
        down[at] = dot_rows(hidden[:, at], out_grad[...]).astype(jnp.bfloat16)
        copy = pltpu.make_async_copy(down.at[at], down_ref.at[at], sem.at[len(copies)])
        copy.start()
        copies.append(copy)
    ig_ref[...] = ig_in[...]
    peak_ref[0] = peak_in[0]
    peak_ref[1] = peak_in[1]
    for copy in copies:
        copy.wait()


def local(tokens, gate_weight, up_weight, down_weight, out_grad):
    bf16, f32 = jnp.bfloat16, jnp.float32
    width, hid = gate_weight.shape
    group, size = 2 * NX * ROWS, NY * ROWS
    total = 2 * NX * size
    anywhere = pl.BlockSpec(memory_space=pl.ANY)
    vmem, dma = pltpu.VMEM, pltpu.SemaphoreType.DMA
    args = [pltpu.with_memory_space_constraint(v, pltpu.HBM) for v in (tokens, out_grad, gate_weight, up_weight, down_weight)]
    input_grad, peaks, gate_grad, up_grad, hidden, grad_all = pl.pallas_call(
        main_kernel,
        name="slab",
        out_shape=(
            jax.ShapeDtypeStruct((ROWS, width), bf16),
            jax.ShapeDtypeStruct((2,), f32),
            jax.ShapeDtypeStruct((width, hid), bf16),
            jax.ShapeDtypeStruct((width, hid), bf16),
            jax.ShapeDtypeStruct((2 * NX, size, hid), bf16),
            jax.ShapeDtypeStruct((2 * NX, size, width), bf16),
        ),
        in_specs=[pl.BlockSpec(memory_space=pltpu.HBM)] * 5,
        out_specs=(
            pl.BlockSpec(memory_space=pltpu.VMEM),
            pl.BlockSpec(memory_space=pltpu.SMEM),
            anywhere,
            anywhere,
            anywhere,
            anywhere,
        ),
        scratch_shapes=[
            vmem((2, 2 * NX, size, width), bf16),
            vmem((width, hid), bf16),
            vmem((width, hid), bf16),
            vmem((hid, width), bf16),
            vmem((width, hid), bf16),
            vmem((hid, width), bf16),
            vmem((hid, width), bf16),
            vmem((NY, 3, group, hid), f32),
            vmem((2, NY, 4, 3, ROWS, hid), bf16),
            vmem((2, NY, 4, 3, ROWS, hid), bf16),
            vmem((3, 2 * NX, size, hid), bf16),
            vmem((2, 2 * NX, size, hid), bf16),
            vmem((2, width, hid), bf16),
            vmem((NY, NZ * ROWS, width), bf16),
            vmem((NY, NZ * ROWS, width), bf16),
            vmem((NZ * ROWS, width), bf16),
            vmem((8, ROWS, width), bf16),
            vmem((4, 16, 128), f32),
            vmem((17, 16, 128), f32),
            dma((5,)),
            dma((2, 3)), dma((2, 3)), dma((2, 4)), dma((2, 4)), dma((2, 3, 4)), dma((2, 3, 4)), dma((2, 3)), dma((2, 3)),
            dma((2, NY, 4, 2)), dma((2, NY, 4, 2)), dma((2, NY, 4)), dma((2, NY, 4)), dma((2, 2, 4)), dma((2, 2, 4)),
            dma((17,)), dma((17,)), dma((4, 3)), dma((4, 3)), dma((8,)), dma((8,)), dma((4,)),
        ],
        compiler_params=pltpu.CompilerParams(collective_id=0, has_side_effects=True, vmem_limit_bytes=40 * 2**20),
    )(*args)
    whole = pl.BlockSpec(memory_space=pltpu.VMEM)
    smem = pl.BlockSpec(memory_space=pltpu.SMEM)
    gate_grad, up_grad, down_grad, input_grad, peaks = pl.pallas_call(
        weight_kernel,
        name="weight_grads",
        out_shape=(
            jax.ShapeDtypeStruct((width, hid), bf16),
            jax.ShapeDtypeStruct((width, hid), bf16),
            jax.ShapeDtypeStruct((hid, width), bf16),
            jax.ShapeDtypeStruct((ROWS, width), bf16),
            jax.ShapeDtypeStruct((2,), f32),
        ),
        in_specs=[anywhere, anywhere, whole, whole, whole, smem],
        out_specs=(anywhere, anywhere, anywhere, whole, smem),
        scratch_shapes=[vmem((hid, width), bf16), dma((8,))],
        compiler_params=pltpu.CompilerParams(vmem_limit_bytes=16 * 2**20),
    )(gate_grad, up_grad, hidden.reshape(total, hid), grad_all.reshape(total, width), input_grad, peaks)
    return input_grad, gate_grad, up_grad, down_grad, peaks


def solution(mesh):
    in_specs = (P("gy", "gx"), P("gx", "gy"), P("gx", "gy"), P("gy", "gx"), P("gy", "gx"))
    out_specs = (P("gy", "gx"), P("gx", "gy"), P("gx", "gy"), P("gy", "gx"), P())
    return jax.shard_map(local, mesh=mesh, in_specs=in_specs, out_specs=out_specs, check_vma=False)
```

```python
import functools

import jax
import jax.numpy as jnp
from jax import lax
from jax.experimental import pallas as pl
from jax.experimental.pallas import tpu as pltpu
from jax.sharding import PartitionSpec as P

MESH = pl.DeviceIdType.MESH
FP8_MAX = 57344.0
HEADROOM = 8.0
TOP = HEADROOM * FP8_MAX
NZ, NY, NX, ROWS = 8, 4, 4, 16
GROUPS = (0, 1, 3, 2)
FIRST = 0
GATE, UP, HGRAD = 0, 1, 2
PRE_GATE, PRE_UP, HIDDEN = 0, 1, 2


def dot(a, b):
    return jnp.dot(a, b, preferred_element_type=jnp.float32)


def dot_rows(a, b):
    return lax.dot_general(a, b, (((0,), (0,)), ((), ())), preferred_element_type=jnp.float32)


def device(z, y, x, c):
    return (lax.rem(z + NZ, NZ), (lax.rem(y + NY, NY) * NX + lax.rem(x + NX, NX)) * 2 + c)


def main_kernel(
    tok_hbm, grad_hbm, wg_hbm, wu_hbm, wd_hbm,
    ig_ref, peak_ref, gate_out, up_out, hidden_out, grad_out,
    xy, wg, wu, wd, wdt, wgt, wut, part, rs_send, rs_recv, back, coded, w_grad, ig_part, ig_core, ig_sum, ig_recv, row_sum, row_recv,
    pk, pk_recv,
    w_sem, x_send, x_recv, f_send, f_recv, y_send, y_recv, g_send, g_recv,
    r_send, r_recv, a_send, a_recv, h_send, h_recv, p_send, p_recv, b_send, b_recv, c_send, c_recv, d_send, d_recv, o_sem,
):
    z, gy = lax.axis_index("gx"), lax.axis_index("gy")
    y, x, c = gy // 8, lax.rem(gy // 2, NX), lax.rem(gy, 2)
    mine = c * NX + x
    partner = device(z, y, x, 1 - c)
    ups = (device(z + 1, y, x, c), device(z - 1, y, x, c))
    sends, outs = [], []

    def remote(src, dst, s_sem, r_sem, dev):
        return pltpu.make_async_remote_copy(
            src_ref=src, dst_ref=dst, send_sem=s_sem, recv_sem=r_sem, device_id=dev, device_id_type=MESH
        )

    def send(src, dst, s_sem, r_sem, dev):
        copy = remote(src, dst, s_sem, r_sem, dev)
        copy.start()
        sends.append(copy)

    def arrived(ref, s_sem, r_sem):
        remote(ref, ref, s_sem, r_sem, partner).wait_recv()

    def rows(j, n=1):
        return pl.ds(pl.multiple_of(j * ROWS, ROWS), n * ROWS)

    def of(d, n=1):
        return slice(d * ROWS, (d + n) * ROWS)

    def chunk(k):
        return lax.rem(z + k + 2 * NZ, NZ)

    w_copies = [
        pltpu.make_async_copy(src, dst, w_sem.at[i])
        for i, (src, dst) in enumerate(
            ((tok_hbm, xy.at[0, mine, of(0)]), (grad_hbm, xy.at[1, mine, of(0)]), (wd_hbm, wd), (wg_hbm, wg), (wu_hbm, wu))
        )
    ]
    for copy in w_copies:
        copy.start()

    barrier = pltpu.get_barrier_semaphore()
    greet = [partner, *ups]
    greet += [device(z, y, x + i, c) for i in (1, 2, 3)] + [device(z, y + i, x, c) for i in (1, 2, 3)]
    for dev in greet:
        pl.semaphore_signal(barrier, inc=1, device_id=dev, device_id_type=MESH)
    w_copies[0].wait()
    w_copies[1].wait()
    pl.semaphore_wait(barrier, len(greet))

    def row_send(a):
        ref = xy.at[a, mine, of(0)]
        for i in (1, 3, 2):
            send(ref, ref, x_send.at[a, i - 1], x_recv.at[a, i - 1], device(z, y, x + i, c))
        send(ref, ref, f_send.at[a, 0], f_recv.at[a, 0], partner)

    def column_send(a, piece, dists):
        j = c * NX + lax.rem(x - piece + NX, NX)
        for i in dists:
            send(
                xy.at[a, j, of(0)], xy.at[a, j, of(4 - i)], y_send.at[a, i - 1, piece], y_recv.at[a, i - 1, piece],
                device(z, y + i, x, c),
            )

    def row_forward(a, i):
        ref = xy.at[a, c * NX + lax.rem(x - i + NX, NX), of(0)]
        arrived(ref, x_send.at[a, i - 1], x_recv.at[a, i - 1])
        send(ref, ref, f_send.at[a, i], f_recv.at[a, i], partner)
        column_send(a, i, (1, 3))

    def column_far(a):
        for piece in range(4):
            column_send(a, piece, (2,))

    def row_done(a):
        for i in range(4):
            ref = xy.at[a, (1 - c) * NX + lax.rem(x - i + NX, NX), of(0)]
            arrived(ref, f_send.at[a, i], f_recv.at[a, i])

    def half(a, d, core):
        return xy.at[a, pl.ds(core * NX, NX), of(d)]

    def column_forward(a, i):
        for piece in (0, 1, 3, 2):
            ref = xy.at[a, c * NX + lax.rem(x - piece + NX, NX), of(4 - i)]
            arrived(ref, y_send.at[a, i - 1, piece], y_recv.at[a, i - 1, piece])
        ref = half(a, 4 - i, c)
        send(ref, ref, g_send.at[a, i - 1], g_recv.at[a, i - 1], partner)

    def column_done(a, d):
        if d:
            arrived(half(a, d, 1 - c), g_send.at[a, 3 - d], g_recv.at[a, 3 - d])

    def group(a, d):
        return xy[a, :, of(d)].reshape(2 * NX * ROWS, xy.shape[3])

    def transpose_down():
        w_copies[2].wait()
        wdt[...] = wd[...].T

    def transpose_gate():
        wgt[...] = wg[...].T

    def transpose_up():
        wut[...] = wu[...].T

    def forward_products(d):
        if d == 0:
            w_copies[3].wait()
            w_copies[4].wait()
        column_done(0, d)
        part[d, GATE] = dot(group(0, d), wg[...])
        part[d, UP] = dot(group(0, d), wu[...])

    def grad_products(d):
        column_done(1, d)
        part[d, HGRAD] = dot(group(1, d), wdt[...])

    def span(kind, s, side, d):
        if kind == "gu":
            return (0, 2) if s else ((0, 1), (1, 2))[side]
        return (2, 3) if s or (side == 0) == (d in GROUPS[:2]) else None

    def reduce_step(kind, d, s):
        k = 0 if kind == "gu" else 1
        for side in (0, 1):
            now = span(kind, s, side, d)
            if now is None:
                continue
            j = chunk(4 - s if side == 0 else s - 4)
            before = span(kind, s - 1, side, d) if s else None
            if before is not None:
                lo, hi = before
                arrived(rs_recv.at[side, d, s - 1, lo:hi], r_send.at[side, d, s - 1, k], r_recv.at[side, d, s - 1, k])
            for a in range(*now):
                total = part[d, a, rows(j)]
                if before is not None and before[0] <= a < before[1]:
                    total += rs_recv[side, d, s - 1, a].astype(jnp.float32)
                rs_send[side, d, s, a] = total.astype(jnp.bfloat16)
            lo, hi = now
            send(
                rs_send.at[side, d, s, lo:hi], rs_recv.at[side, d, s, lo:hi],
                r_send.at[side, d, s, k], r_recv.at[side, d, s, k], ups[side],
            )

    def finish(d):
        for side in (0, 1):
            arrived(rs_recv.at[side, d, 3, 0:2], r_send.at[side, d, 3, 0], r_recv.at[side, d, 3, 0])
            arrived(rs_recv.at[side, d, 3, 2:3], r_send.at[side, d, 3, 1], r_recv.at[side, d, 3, 1])
        total = [
            part[d, a, rows(z)] + rs_recv[0, d, 3, a].astype(jnp.float32) + rs_recv[1, d, 3, a].astype(jnp.float32)
            for a in range(3)
        ]
        gate, up_val, hidden_grad = total
        sigma = jax.nn.sigmoid(gate)
        act = gate * sigma
        slope = sigma * (1.0 + gate * (1.0 - sigma))
        pre_gate = hidden_grad * up_val * slope
        pre_up = hidden_grad * act
        back[PRE_GATE, z, of(d)] = pre_gate.astype(jnp.bfloat16)
        back[PRE_UP, z, of(d)] = pre_up.astype(jnp.bfloat16)
        back[HIDDEN, z, of(d)] = (act * up_val).astype(jnp.bfloat16)
        for i, values in enumerate((pre_gate, pre_up)):
            top = jnp.abs(values)
            top = jnp.max(top.reshape(2, 8, top.shape[1]), axis=0)
            best = top[:, 0:128]
            for k in range(1, top.shape[1] // 128):
                best = jnp.maximum(best, top[:, k * 128 : (k + 1) * 128])
            if d != FIRST:
                best = jnp.maximum(best, pk[0, i * 8 : i * 8 + 8])
            pk[0, i * 8 : i * 8 + 8] = best

    def spread_ref(d, t, side):
        j = chunk(-t if side == 0 else t)
        lo, hi = (0, 2) if t < 3 else (side, side + 1)
        return back.at[lo:hi, j, of(d)]

    def landed(d, t):
        for side in (0, 1):
            j = chunk(-t - 1 if side == 0 else t + 1)
            lo, hi = (0, 2) if t < 3 else (side, side + 1)
            arrived(back.at[lo:hi, j, of(d)], a_send.at[side, d, t], a_recv.at[side, d, t])

    def spread(d, t):
        if t:
            landed(d, t - 1)
        for side in (0, 1):
            ref = spread_ref(d, t, side)
            send(ref, ref, a_send.at[side, d, t], a_recv.at[side, d, t], ups[side])

    def hidden_landed(part_of, t):
        for side in (0, 1):
            if t == 3 and side != part_of:
                continue
            j = chunk(-t - 1 if side == 0 else t + 1)
            arrived(back.at[HIDDEN, j, of(2 * part_of, 2)], h_send.at[side, part_of, t], h_recv.at[side, part_of, t])

    def hidden_spread(part_of, t):
        if t:
            hidden_landed(part_of, t - 1)
        for side in (0, 1):
            if t == 3 and side != part_of:
                continue
            ref = back.at[HIDDEN, chunk(-t if side == 0 else t), of(2 * part_of, 2)]
            send(ref, ref, h_send.at[side, part_of, t], h_recv.at[side, part_of, t], ups[side])

    row_devs = [device(z, y, x + i % 4, c if i < 4 else 1 - c) for i in range(1, 8)]
    col_devs = [device(z, y + i, x, c) for i in range(1, 4)]
    z_devs = [device(z + i, y, x, c) for i in range(1, 8)]
    stages = ((0, row_devs), (7, col_devs), (10, z_devs))

    def peaks_send(stage):
        first, devs = stages[stage]
        for i, dev in enumerate(devs):
            send(pk.at[stage], pk_recv.at[first + i], p_send.at[first + i], p_recv.at[first + i], dev)

    def peaks_wait(stage):
        first, devs = stages[stage]
        best = pk[stage]
        for i in range(len(devs)):
            arrived(pk_recv.at[first + i], p_send.at[first + i], p_recv.at[first + i])
        for i in range(len(devs)):
            best = jnp.maximum(best, pk_recv[first + i])
        pk[stage + 1] = best

    def safe_peaks():
        return jnp.max(pk[3, 0:8]) + 1e-6, jnp.max(pk[3, 8:16]) + 1e-6

    parts = ((0, 1, -1), (2, -2), (3, -3), (4,))
    starts = (0, 3, 5, 7)

    def input_products(q):
        peaks = safe_peaks()
        size = 4 * ROWS
        for i, which in enumerate((PRE_GATE, PRE_UP)):
            scale = TOP / peaks[i]
            for k in parts[q]:
                j = chunk(k)
                values = back[which, j].astype(jnp.float32) * scale
                coded[i, j] = jnp.clip(values, -FP8_MAX, FP8_MAX).astype(jnp.bfloat16)
        first, second = (
            dot(jnp.concatenate([coded[i, chunk(k)] for k in parts[q]], axis=0), w[...]) for i, w in enumerate((wgt, wut))
        )
        total = ((peaks[0] / TOP) * first + (peaks[1] / TOP) * second).astype(jnp.bfloat16)
        for m in range(len(parts[q])):
            for d in range(4):
                ig_part[d // 2, d % 2, of(starts[q] + m)] = total[m * size + d * ROWS : m * size + (d + 1) * ROWS]

    def core_sum_send(q):
        at = of(starts[q], len(parts[q]))
        send(ig_part.at[:, 1 - c, at], ig_core.at[:, at], b_send.at[q], b_recv.at[q], partner)

    def column_copy(q, i):
        at = of(starts[q], len(parts[q]))
        dev = device(z, y + 2 * i + c, x, c)
        return remote(ig_sum.at[i, at], ig_recv.at[i, at], c_send.at[q, i], c_recv.at[q, i], dev)

    def column_sum_send(q):
        at = of(starts[q], len(parts[q]))
        arrived(ig_core.at[:, at], b_send.at[q], b_recv.at[q])
        for i in (1, 0):
            total = ig_part[i, c, at].astype(jnp.float32) + ig_core[i, at].astype(jnp.float32)
            ig_sum[i, at] = total.astype(jnp.bfloat16)
            copy = column_copy(q, i)
            if i:
                copy.start()
                continue

            @pl.when(c == 1)
            def _():
                copy.start()

            @pl.when(c == 0)
            def _():
                ig_recv[0, at] = ig_sum[0, at]

    def column_sum_sent():
        for q in range(4):
            column_copy(q, 1).wait_send()

            @pl.when(c == 1)
            def _():
                column_copy(q, 0).wait_send()

    def row_copy(q, m):
        j = chunk(parts[q][m])
        ref = row_sum.at[of(starts[q] + m)]
        k = starts[q] + m
        return j, ref, remote(ref, row_recv.at[mine], d_send.at[k], d_recv.at[mine], device(z, y, lax.rem(j, NX), j // NX))

    def row_sum_send(q):
        at = of(starts[q], len(parts[q]))
        arrived(ig_recv.at[1, at], c_send.at[q, 1], c_recv.at[q, 1])

        @pl.when(c == 1)
        def _():
            arrived(ig_recv.at[0, at], c_send.at[q, 0], c_recv.at[q, 0])

        total = ig_recv[0, at].astype(jnp.float32) + ig_recv[1, at].astype(jnp.float32)
        row_sum[at] = total.astype(jnp.bfloat16)
        for m in range(len(parts[q])):
            j, ref, copy = row_copy(q, m)

            @pl.when(j != mine)
            def _():
                copy.start()

            @pl.when(j == mine)
            def _():
                row_recv[mine] = ref[...]

    def row_sum_finish():
        for i in range(1, 8):
            src = lax.rem(mine + i, 8)
            arrived(row_recv.at[src], d_send.at[0], d_recv.at[src])
        total = row_recv[0].astype(jnp.float32)
        for i in range(1, 8):
            total += row_recv[i].astype(jnp.float32)
        ig_ref[...] = total.astype(jnp.bfloat16)

    def row_sum_sent():
        for q in range(4):
            for m in range(len(parts[q])):
                j, _, copy = row_copy(q, m)

                @pl.when(j != mine)
                def _():
                    copy.wait_send()

    def weight_products(i):
        scale = safe_peaks()[i] / TOP
        width = xy.shape[3]
        total = 2 * NX * 4 * ROWS
        right = coded[i].reshape(total, coded.shape[3])
        for k in range(0, width, 256):
            left = xy[0, :, :, k : k + 256].reshape(total, 256)
            w_grad[i, k : k + 256] = (scale * dot_rows(left, right)).astype(jnp.bfloat16)
        copy = pltpu.make_async_copy(w_grad.at[i], (gate_out, up_out)[i], o_sem.at[i])
        copy.start()
        outs.append(copy)

    def out(src, dst, sem):
        copy = pltpu.make_async_copy(src, dst, o_sem.at[sem])
        copy.start()
        outs.append(copy)

    row_send(0)
    column_send(0, 0, (1, 3))
    row_send(1)
    column_send(1, 0, (1, 3))
    row_forward(0, 3)
    row_forward(0, 1)
    transpose_down()
    row_forward(0, 2)
    column_far(0)
    row_forward(1, 1)
    row_forward(1, 3)
    row_done(0)
    forward_products(0)
    row_forward(1, 2)
    reduce_step("gu", 0, 0)
    column_forward(0, 1)
    column_forward(0, 3)
    row_done(1)
    grad_products(0)
    reduce_step("hg", 0, 0)
    forward_products(3)
    reduce_step("gu", 3, 0)
    reduce_step("gu", 0, 1)
    forward_products(1)
    reduce_step("hg", 0, 1)
    reduce_step("gu", 1, 0)
    column_forward(1, 1)
    column_forward(1, 3)
    reduce_step("gu", 3, 1)
    column_forward(0, 2)
    column_far(1)
    reduce_step("gu", 0, 2)
    grad_products(3)
    reduce_step("hg", 0, 2)
    reduce_step("hg", 3, 0)
    reduce_step("gu", 1, 1)
    grad_products(1)
    reduce_step("gu", 3, 2)
    reduce_step("gu", 0, 3)
    forward_products(2)
    reduce_step("gu", 2, 0)
    reduce_step("hg", 1, 0)
    reduce_step("hg", 3, 1)
    column_forward(1, 2)
    reduce_step("gu", 1, 2)
    grad_products(2)
    out(xy.at[1], grad_out, 3)
    reduce_step("hg", 2, 0)
    reduce_step("hg", 0, 3)
    reduce_step("hg", 1, 1)
    reduce_step("gu", 2, 1)
    reduce_step("hg", 3, 2)
    reduce_step("hg", 2, 1)
    reduce_step("gu", 3, 3)
    reduce_step("hg", 1, 2)
    reduce_step("gu", 2, 2)
    reduce_step("hg", 2, 2)
    finish(0)
    reduce_step("gu", 1, 3)
    reduce_step("hg", 3, 3)
    reduce_step("hg", 1, 3)
    reduce_step("gu", 2, 3)
    reduce_step("hg", 2, 3)
    finish(3)
    spread(0, 0)
    finish(1)
    spread(1, 0)
    spread(3, 0)
    finish(2)
    peaks_send(0)
    spread(2, 0)
    hidden_spread(1, 0)
    spread(3, 1)
    spread(1, 1)
    peaks_wait(0)
    peaks_send(1)
    spread(0, 1)
    spread(2, 1)
    peaks_wait(1)
    peaks_send(2)
    spread(1, 2)
    spread(3, 2)
    spread(0, 2)
    spread(2, 2)
    spread(1, 3)
    hidden_spread(0, 0)
    transpose_gate()
    transpose_up()
    spread(3, 3)
    hidden_spread(1, 1)
    peaks_wait(2)
    input_products(0)
    core_sum_send(0)
    spread(0, 3)
    input_products(1)
    spread(2, 3)
    column_sum_send(0)
    hidden_spread(0, 1)
    core_sum_send(1)
    input_products(2)
    column_sum_send(1)
    core_sum_send(2)
    hidden_spread(1, 2)
    for d in GROUPS:
        landed(d, 3)
    input_products(3)
    core_sum_send(3)
    column_sum_send(2)
    hidden_spread(0, 2)
    column_sum_send(3)
    row_sum_send(0)
    hidden_spread(1, 3)
    row_sum_send(1)
    hidden_spread(0, 3)
    row_sum_send(2)
    row_sum_send(3)
    weight_products(1)
    weight_products(0)
    hidden_landed(0, 3)
    hidden_landed(1, 3)
    out(back.at[HIDDEN], hidden_out, 2)
    row_sum_finish()
    peak_ref[0] = jnp.max(pk[3, 0:8])
    peak_ref[1] = jnp.max(pk[3, 8:16])
    column_sum_sent()
    row_sum_sent()
    for copy in outs:
        copy.wait()
    for copy in sends:
        copy.wait_send()


def weight_kernel(gate_in, up_in, hidden, out_grad, ig_in, peak_in, gate_ref, up_ref, down_ref, ig_ref, peak_ref, down, sem):
    copies = []

    def store(src, dst):
        copy = pltpu.make_async_copy(src, dst, sem.at[len(copies)])
        copy.start()
        copies.append(copy)

    for k in range(0, gate_in.shape[0], 256):
        store(gate_in.at[k : k + 256], gate_ref.at[k : k + 256])
        store(up_in.at[k : k + 256], up_ref.at[k : k + 256])
    for k in range(0, down.shape[0], 128):
        down[k : k + 128] = dot_rows(hidden[:, k : k + 128], out_grad[...]).astype(jnp.bfloat16)
        store(down.at[k : k + 128], down_ref.at[k : k + 128])
    ig_ref[...] = ig_in[...]
    peak_ref[0] = peak_in[0]
    peak_ref[1] = peak_in[1]
    for copy in copies:
        copy.wait()


def local(tokens, gate_weight, up_weight, down_weight, out_grad):
    bf16, f32 = jnp.bfloat16, jnp.float32
    width, hid = gate_weight.shape
    group, size = 2 * NX * ROWS, NY * ROWS
    total = 2 * NX * size
    anywhere = pl.BlockSpec(memory_space=pl.ANY)
    vmem, dma = pltpu.VMEM, pltpu.SemaphoreType.DMA
    args = [pltpu.with_memory_space_constraint(v, pltpu.HBM) for v in (tokens, out_grad, gate_weight, up_weight, down_weight)]
    input_grad, peaks, gate_grad, up_grad, hidden, grad_all = pl.pallas_call(
        main_kernel,
        name="slab",
        out_shape=(
            jax.ShapeDtypeStruct((ROWS, width), bf16),
            jax.ShapeDtypeStruct((2,), f32),
            jax.ShapeDtypeStruct((width, hid), bf16),
            jax.ShapeDtypeStruct((width, hid), bf16),
            jax.ShapeDtypeStruct((2 * NX, size, hid), bf16),
            jax.ShapeDtypeStruct((2 * NX, size, width), bf16),
        ),
        in_specs=[pl.BlockSpec(memory_space=pltpu.HBM)] * 5,
        out_specs=(
            pl.BlockSpec(memory_space=pltpu.VMEM),
            pl.BlockSpec(memory_space=pltpu.SMEM),
            anywhere,
            anywhere,
            anywhere,
            anywhere,
        ),
        scratch_shapes=[
            vmem((2, 2 * NX, size, width), bf16),
            vmem((width, hid), bf16),
            vmem((width, hid), bf16),
            vmem((hid, width), bf16),
            vmem((width, hid), bf16),
            vmem((hid, width), bf16),
            vmem((hid, width), bf16),
            vmem((NY, 3, group, hid), f32),
            vmem((2, NY, 4, 3, ROWS, hid), bf16),
            vmem((2, NY, 4, 3, ROWS, hid), bf16),
            vmem((3, 2 * NX, size, hid), bf16),
            vmem((2, 2 * NX, size, hid), bf16),
            vmem((2, width, hid), bf16),
            vmem((2, 2, NZ * ROWS, width), bf16),
            vmem((2, NZ * ROWS, width), bf16),
            vmem((2, NZ * ROWS, width), bf16),
            vmem((2, NZ * ROWS, width), bf16),
            vmem((NZ * ROWS, width), bf16),
            vmem((8, ROWS, width), bf16),
            vmem((4, 16, 128), f32),
            vmem((17, 16, 128), f32),
            dma((5,)),
            dma((2, 3)), dma((2, 3)), dma((2, 4)), dma((2, 4)), dma((2, 3, 4)), dma((2, 3, 4)), dma((2, 3)), dma((2, 3)),
            dma((2, NY, 4, 2)), dma((2, NY, 4, 2)), dma((2, NY, 4)), dma((2, NY, 4)), dma((2, 2, 4)), dma((2, 2, 4)),
            dma((17,)), dma((17,)), dma((4,)), dma((4,)), dma((4, 2)), dma((4, 2)), dma((8,)), dma((8,)), dma((5,)),
        ],
        compiler_params=pltpu.CompilerParams(collective_id=0, has_side_effects=True, vmem_limit_bytes=40 * 2**20),
    )(*args)
    whole = pl.BlockSpec(memory_space=pltpu.VMEM)
    smem = pl.BlockSpec(memory_space=pltpu.SMEM)
    gate_grad, up_grad, down_grad, input_grad, peaks = pl.pallas_call(
        weight_kernel,
        name="weight_grads",
        out_shape=(
            jax.ShapeDtypeStruct((width, hid), bf16),
            jax.ShapeDtypeStruct((width, hid), bf16),
            jax.ShapeDtypeStruct((hid, width), bf16),
            jax.ShapeDtypeStruct((ROWS, width), bf16),
            jax.ShapeDtypeStruct((2,), f32),
        ),
        in_specs=[anywhere, anywhere, whole, whole, whole, smem],
        out_specs=(anywhere, anywhere, anywhere, whole, smem),
        scratch_shapes=[vmem((hid, width), bf16), dma((16,))],
        compiler_params=pltpu.CompilerParams(vmem_limit_bytes=16 * 2**20),
    )(gate_grad, up_grad, hidden.reshape(total, hid), grad_all.reshape(total, width), input_grad, peaks)
    return input_grad, gate_grad, up_grad, down_grad, peaks


def solution(mesh):
    in_specs = (P("gy", "gx"), P("gx", "gy"), P("gx", "gy"), P("gy", "gx"), P("gy", "gx"))
    out_specs = (P("gy", "gx"), P("gx", "gy"), P("gx", "gy"), P("gy", "gx"), P())
    return jax.shard_map(local, mesh=mesh, in_specs=in_specs, out_specs=out_specs, check_vma=False)
```

```python
import functools

import jax
import jax.numpy as jnp
from jax import lax
from jax.experimental import pallas as pl
from jax.experimental.pallas import tpu as pltpu
from jax.sharding import PartitionSpec as P

MESH = pl.DeviceIdType.MESH
FP8_MAX = 57344.0
HEADROOM = 8.0
TOP = HEADROOM * FP8_MAX
NZ, NY, NX, ROWS = 8, 4, 4, 16
GROUPS = (0, 1, 3, 2)
FIRST = 0
GATE, UP, HGRAD = 0, 1, 2
PRE_GATE, PRE_UP, HIDDEN = 0, 1, 2


def dot(a, b):
    return jnp.dot(a, b, preferred_element_type=jnp.float32)


def dot_rows(a, b):
    return lax.dot_general(a, b, (((0,), (0,)), ((), ())), preferred_element_type=jnp.float32)


def device(z, y, x, c):
    return (lax.rem(z + NZ, NZ), (lax.rem(y + NY, NY) * NX + lax.rem(x + NX, NX)) * 2 + c)


def main_kernel(
    tok_hbm, grad_hbm, wg_hbm, wu_hbm, wd_hbm,
    ig_ref, peak_ref, gate_out, up_out, hidden_out, grad_out,
    xy, wg, wu, wd, wdt, wgt, wut, part, rs_send, rs_recv, back, coded, w_grad, ig_part, ig_core, ig_sum, ig_recv, row_sum, row_recv,
    pk, pk_recv,
    w_sem, x_send, x_recv, f_send, f_recv, y_send, y_recv, g_send, g_recv,
    r_send, r_recv, a_send, a_recv, h_send, h_recv, p_send, p_recv, b_send, b_recv, c_send, c_recv, d_send, d_recv, o_sem,
):
    z, gy = lax.axis_index("gx"), lax.axis_index("gy")
    y, x, c = gy // 8, lax.rem(gy // 2, NX), lax.rem(gy, 2)
    mine = c * NX + x
    partner = device(z, y, x, 1 - c)
    ups = (device(z + 1, y, x, c), device(z - 1, y, x, c))
    sends, outs = [], []

    def remote(src, dst, s_sem, r_sem, dev):
        return pltpu.make_async_remote_copy(
            src_ref=src, dst_ref=dst, send_sem=s_sem, recv_sem=r_sem, device_id=dev, device_id_type=MESH
        )

    def send(src, dst, s_sem, r_sem, dev):
        copy = remote(src, dst, s_sem, r_sem, dev)
        copy.start()
        sends.append(copy)

    def arrived(ref, s_sem, r_sem):
        remote(ref, ref, s_sem, r_sem, partner).wait_recv()

    def rows(j, n=1):
        return pl.ds(pl.multiple_of(j * ROWS, ROWS), n * ROWS)

    def of(d, n=1):
        return slice(d * ROWS, (d + n) * ROWS)

    def chunk(k):
        return lax.rem(z + k + 2 * NZ, NZ)

    w_copies = [
        pltpu.make_async_copy(src, dst, w_sem.at[i])
        for i, (src, dst) in enumerate(
            ((tok_hbm, xy.at[0, mine, of(0)]), (grad_hbm, xy.at[1, mine, of(0)]), (wd_hbm, wd), (wg_hbm, wg), (wu_hbm, wu))
        )
    ]
    for copy in w_copies:
        copy.start()

    barrier = pltpu.get_barrier_semaphore()
    greet = [partner, *ups]
    greet += [device(z, y, x + i, c) for i in (1, 2, 3)] + [device(z, y + i, x, c) for i in (1, 2, 3)]
    for dev in greet:
        pl.semaphore_signal(barrier, inc=1, device_id=dev, device_id_type=MESH)
    w_copies[0].wait()
    w_copies[1].wait()
    pl.semaphore_wait(barrier, len(greet))

    def row_send(a):
        ref = xy.at[a, mine, of(0)]
        for i in (1, 3, 2):
            send(ref, ref, x_send.at[a, i - 1], x_recv.at[a, i - 1], device(z, y, x + i, c))
        send(ref, ref, f_send.at[a, 0], f_recv.at[a, 0], partner)

    def column_send(a, piece, dists):
        j = c * NX + lax.rem(x - piece + NX, NX)
        for i in dists:
            send(
                xy.at[a, j, of(0)], xy.at[a, j, of(4 - i)], y_send.at[a, i - 1, piece], y_recv.at[a, i - 1, piece],
                device(z, y + i, x, c),
            )

    def row_forward(a, i):
        ref = xy.at[a, c * NX + lax.rem(x - i + NX, NX), of(0)]
        arrived(ref, x_send.at[a, i - 1], x_recv.at[a, i - 1])
        send(ref, ref, f_send.at[a, i], f_recv.at[a, i], partner)
        column_send(a, i, (1, 3))

    def column_far(a):
        for piece in range(4):
            column_send(a, piece, (2,))

    def row_done(a):
        for i in range(4):
            ref = xy.at[a, (1 - c) * NX + lax.rem(x - i + NX, NX), of(0)]
            arrived(ref, f_send.at[a, i], f_recv.at[a, i])

    def half(a, d, core):
        return xy.at[a, pl.ds(core * NX, NX), of(d)]

    def column_forward(a, i):
        for piece in (0, 1, 3, 2):
            ref = xy.at[a, c * NX + lax.rem(x - piece + NX, NX), of(4 - i)]
            arrived(ref, y_send.at[a, i - 1, piece], y_recv.at[a, i - 1, piece])
        ref = half(a, 4 - i, c)
        send(ref, ref, g_send.at[a, i - 1], g_recv.at[a, i - 1], partner)

    def column_done(a, d):
        if d:
            arrived(half(a, d, 1 - c), g_send.at[a, 3 - d], g_recv.at[a, 3 - d])

    def group(a, d):
        return xy[a, :, of(d)].reshape(2 * NX * ROWS, xy.shape[3])

    def transpose_down():
        w_copies[2].wait()
        wdt[...] = wd[...].T

    def transpose_gate():
        wgt[...] = wg[...].T

    def transpose_up():
        wut[...] = wu[...].T

    def forward_products(d):
        if d == 0:
            w_copies[3].wait()
            w_copies[4].wait()
        column_done(0, d)
        part[d, GATE] = dot(group(0, d), wg[...])
        part[d, UP] = dot(group(0, d), wu[...])

    def grad_products(d):
        column_done(1, d)
        part[d, HGRAD] = dot(group(1, d), wdt[...])

    def span(kind, s, side, d):
        if kind == "gu":
            return (0, 2) if s else ((0, 1), (1, 2))[side]
        return (2, 3) if s or (side == 0) == (d in GROUPS[:2]) else None

    def reduce_step(kind, d, s):
        k = 0 if kind == "gu" else 1
        for side in (0, 1):
            now = span(kind, s, side, d)
            if now is None:
                continue
            j = chunk(4 - s if side == 0 else s - 4)
            before = span(kind, s - 1, side, d) if s else None
            if before is not None:
                lo, hi = before
                arrived(rs_recv.at[side, d, s - 1, lo:hi], r_send.at[side, d, s - 1, k], r_recv.at[side, d, s - 1, k])
            for a in range(*now):
                total = part[d, a, rows(j)]
                if before is not None and before[0] <= a < before[1]:
                    total += rs_recv[side, d, s - 1, a].astype(jnp.float32)
                rs_send[side, d, s, a] = total.astype(jnp.bfloat16)
            lo, hi = now
            send(
                rs_send.at[side, d, s, lo:hi], rs_recv.at[side, d, s, lo:hi],
                r_send.at[side, d, s, k], r_recv.at[side, d, s, k], ups[side],
            )

    def finish(d):
        for side in (0, 1):
            arrived(rs_recv.at[side, d, 3, 0:2], r_send.at[side, d, 3, 0], r_recv.at[side, d, 3, 0])
            arrived(rs_recv.at[side, d, 3, 2:3], r_send.at[side, d, 3, 1], r_recv.at[side, d, 3, 1])
        total = [
            part[d, a, rows(z)] + rs_recv[0, d, 3, a].astype(jnp.float32) + rs_recv[1, d, 3, a].astype(jnp.float32)
            for a in range(3)
        ]
        gate, up_val, hidden_grad = total
        sigma = jax.nn.sigmoid(gate)
        act = gate * sigma
        slope = sigma * (1.0 + gate * (1.0 - sigma))
        pre_gate = hidden_grad * up_val * slope
        pre_up = hidden_grad * act
        back[PRE_GATE, z, of(d)] = pre_gate.astype(jnp.bfloat16)
        back[PRE_UP, z, of(d)] = pre_up.astype(jnp.bfloat16)
        back[HIDDEN, z, of(d)] = (act * up_val).astype(jnp.bfloat16)
        for i, values in enumerate((pre_gate, pre_up)):
            top = jnp.abs(values)
            top = jnp.max(top.reshape(2, 8, top.shape[1]), axis=0)
            best = top[:, 0:128]
            for k in range(1, top.shape[1] // 128):
                best = jnp.maximum(best, top[:, k * 128 : (k + 1) * 128])
            best = jnp.max(best, axis=0, keepdims=True)
            if d != FIRST:
                best = jnp.maximum(best, pk[0, i : i + 1])
            pk[0, i : i + 1] = best

    def spread_ref(d, t, side):
        j = chunk(-t if side == 0 else t)
        lo, hi = (0, 2) if t < 3 else (side, side + 1)
        return back.at[lo:hi, j, of(d)]

    def landed(d, t):
        for side in (0, 1):
            j = chunk(-t - 1 if side == 0 else t + 1)
            lo, hi = (0, 2) if t < 3 else (side, side + 1)
            arrived(back.at[lo:hi, j, of(d)], a_send.at[side, d, t], a_recv.at[side, d, t])

    def spread(d, t):
        if t:
            landed(d, t - 1)
        for side in (0, 1):
            ref = spread_ref(d, t, side)
            send(ref, ref, a_send.at[side, d, t], a_recv.at[side, d, t], ups[side])

    def hidden_landed(part_of, t):
        for side in (0, 1):
            if t == 3 and side != part_of:
                continue
            j = chunk(-t - 1 if side == 0 else t + 1)
            arrived(back.at[HIDDEN, j, of(2 * part_of, 2)], h_send.at[side, part_of, t], h_recv.at[side, part_of, t])

    def hidden_spread(part_of, t):
        if t:
            hidden_landed(part_of, t - 1)
        for side in (0, 1):
            if t == 3 and side != part_of:
                continue
            ref = back.at[HIDDEN, chunk(-t if side == 0 else t), of(2 * part_of, 2)]
            send(ref, ref, h_send.at[side, part_of, t], h_recv.at[side, part_of, t], ups[side])

    row_devs = [device(z, y, x + i % 4, c if i < 4 else 1 - c) for i in range(1, 8)]
    col_devs = [device(z, y + i, x, c) for i in range(1, 4)]
    z_devs = [device(z + i, y, x, c) for i in range(1, 8)]
    stages = ((0, row_devs), (7, col_devs), (10, z_devs))

    def peaks_send(stage):
        first, devs = stages[stage]
        for i, dev in enumerate(devs):
            send(pk.at[stage], pk_recv.at[first + i], p_send.at[first + i], p_recv.at[first + i], dev)

    def peaks_wait(stage):
        first, devs = stages[stage]
        best = pk[stage]
        for i in range(len(devs)):
            arrived(pk_recv.at[first + i], p_send.at[first + i], p_recv.at[first + i])
        for i in range(len(devs)):
            best = jnp.maximum(best, pk_recv[first + i])
        pk[stage + 1] = best

    def safe_peaks():
        return jnp.max(pk[3, 0:1]) + 1e-6, jnp.max(pk[3, 1:2]) + 1e-6

    parts = ((0, 1, -1), (2, -2), (3, -3), (4,))
    starts = (0, 3, 5, 7)

    def input_products(q):
        peaks = safe_peaks()
        size = 4 * ROWS
        for i, which in enumerate((PRE_GATE, PRE_UP)):
            scale = TOP / peaks[i]
            for k in parts[q]:
                j = chunk(k)
                values = back[which, j].astype(jnp.float32) * scale
                coded[i, j] = jnp.clip(values, -FP8_MAX, FP8_MAX).astype(jnp.bfloat16)
        first, second = (
            dot(jnp.concatenate([coded[i, chunk(k)] for k in parts[q]], axis=0), w[...]) for i, w in enumerate((wgt, wut))
        )
        total = ((peaks[0] / TOP) * first + (peaks[1] / TOP) * second).astype(jnp.bfloat16)
        for m in range(len(parts[q])):
            for d in range(4):
                ig_part[d // 2, d % 2, of(starts[q] + m)] = total[m * size + d * ROWS : m * size + (d + 1) * ROWS]

    def core_sum_send(q):
        at = of(starts[q], len(parts[q]))
        send(ig_part.at[:, 1 - c, at], ig_core.at[:, at], b_send.at[q], b_recv.at[q], partner)

    def column_copy(q, i):
        at = of(starts[q], len(parts[q]))
        dev = device(z, y + 2 * i + c, x, c)
        return remote(ig_sum.at[i, at], ig_recv.at[i, at], c_send.at[q, i], c_recv.at[q, i], dev)

    def column_sum_send(q):
        at = of(starts[q], len(parts[q]))
        arrived(ig_core.at[:, at], b_send.at[q], b_recv.at[q])
        for i in (1, 0):
            total = ig_part[i, c, at].astype(jnp.float32) + ig_core[i, at].astype(jnp.float32)
            ig_sum[i, at] = total.astype(jnp.bfloat16)
            copy = column_copy(q, i)
            if i:
                copy.start()
                continue

            @pl.when(c == 1)
            def _():
                copy.start()

            @pl.when(c == 0)
            def _():
                ig_recv[0, at] = ig_sum[0, at]

    def column_sum_sent():
        for q in range(4):
            column_copy(q, 1).wait_send()

            @pl.when(c == 1)
            def _():
                column_copy(q, 0).wait_send()

    def row_copy(q, m):
        j = chunk(parts[q][m])
        ref = row_sum.at[of(starts[q] + m)]
        k = starts[q] + m
        return j, ref, remote(ref, row_recv.at[mine], d_send.at[k], d_recv.at[mine], device(z, y, lax.rem(j, NX), j // NX))

    def row_sum_send(q):
        at = of(starts[q], len(parts[q]))
        arrived(ig_recv.at[1, at], c_send.at[q, 1], c_recv.at[q, 1])

        @pl.when(c == 1)
        def _():
            arrived(ig_recv.at[0, at], c_send.at[q, 0], c_recv.at[q, 0])

        total = ig_recv[0, at].astype(jnp.float32) + ig_recv[1, at].astype(jnp.float32)
        row_sum[at] = total.astype(jnp.bfloat16)
        for m in range(len(parts[q])):
            j, ref, copy = row_copy(q, m)

            @pl.when(j != mine)
            def _():
                copy.start()

            @pl.when(j == mine)
            def _():
                row_recv[mine] = ref[...]

    def row_sum_finish():
        for i in range(1, 8):
            src = lax.rem(mine + i, 8)
            arrived(row_recv.at[src], d_send.at[0], d_recv.at[src])
        total = row_recv[0].astype(jnp.float32)
        for i in range(1, 8):
            total += row_recv[i].astype(jnp.float32)
        ig_ref[...] = total.astype(jnp.bfloat16)

    def row_sum_sent():
        for q in range(4):
            for m in range(len(parts[q])):
                j, _, copy = row_copy(q, m)

                @pl.when(j != mine)
                def _():
                    copy.wait_send()

    def weight_products(i):
        scale = safe_peaks()[i] / TOP
        width = xy.shape[3]
        total = 2 * NX * 4 * ROWS
        right = coded[i].reshape(total, coded.shape[3])
        for k in range(0, width, 256):
            left = xy[0, :, :, k : k + 256].reshape(total, 256)
            w_grad[i, k : k + 256] = (scale * dot_rows(left, right)).astype(jnp.bfloat16)
        copy = pltpu.make_async_copy(w_grad.at[i], (gate_out, up_out)[i], o_sem.at[i])
        copy.start()
        outs.append(copy)

    def out(src, dst, sem):
        copy = pltpu.make_async_copy(src, dst, o_sem.at[sem])
        copy.start()
        outs.append(copy)

    row_send(0)
    column_send(0, 0, (1, 3))
    row_send(1)
    column_send(1, 0, (1, 3))
    row_forward(0, 3)
    row_forward(0, 1)
    transpose_down()
    row_forward(0, 2)
    column_far(0)
    row_forward(1, 1)
    row_forward(1, 3)
    row_done(0)
    forward_products(0)
    row_forward(1, 2)
    reduce_step("gu", 0, 0)
    column_forward(0, 1)
    column_forward(0, 3)
    row_done(1)
    grad_products(0)
    reduce_step("hg", 0, 0)
    forward_products(3)
    reduce_step("gu", 3, 0)
    reduce_step("gu", 0, 1)
    forward_products(1)
    reduce_step("hg", 0, 1)
    reduce_step("gu", 1, 0)
    column_forward(1, 1)
    column_forward(1, 3)
    reduce_step("gu", 3, 1)
    column_forward(0, 2)
    column_far(1)
    reduce_step("gu", 0, 2)
    grad_products(3)
    reduce_step("hg", 0, 2)
    reduce_step("hg", 3, 0)
    reduce_step("gu", 1, 1)
    grad_products(1)
    reduce_step("gu", 3, 2)
    reduce_step("gu", 0, 3)
    forward_products(2)
    reduce_step("gu", 2, 0)
    reduce_step("hg", 1, 0)
    reduce_step("hg", 3, 1)
    column_forward(1, 2)
    reduce_step("gu", 1, 2)
    grad_products(2)
    out(xy.at[1], grad_out, 3)
    reduce_step("hg", 2, 0)
    reduce_step("hg", 0, 3)
    reduce_step("hg", 1, 1)
    reduce_step("gu", 2, 1)
    reduce_step("hg", 3, 2)
    reduce_step("hg", 2, 1)
    reduce_step("gu", 3, 3)
    reduce_step("hg", 1, 2)
    reduce_step("gu", 2, 2)
    reduce_step("hg", 2, 2)
    finish(0)
    reduce_step("gu", 1, 3)
    reduce_step("hg", 3, 3)
    reduce_step("hg", 1, 3)
    reduce_step("gu", 2, 3)
    reduce_step("hg", 2, 3)
    finish(3)
    spread(0, 0)
    finish(1)
    spread(1, 0)
    spread(3, 0)
    finish(2)
    peaks_send(0)
    spread(2, 0)
    hidden_spread(1, 0)
    spread(3, 1)
    spread(1, 1)
    peaks_wait(0)
    peaks_send(1)
    spread(0, 1)
    spread(2, 1)
    peaks_wait(1)
    peaks_send(2)
    spread(1, 2)
    spread(3, 2)
    spread(0, 2)
    spread(2, 2)
    spread(1, 3)
    hidden_spread(0, 0)
    transpose_gate()
    transpose_up()
    spread(3, 3)
    hidden_spread(1, 1)
    peaks_wait(2)
    input_products(0)
    core_sum_send(0)
    spread(0, 3)
    input_products(1)
    spread(2, 3)
    column_sum_send(0)
    hidden_spread(0, 1)
    core_sum_send(1)
    input_products(2)
    column_sum_send(1)
    core_sum_send(2)
    hidden_spread(1, 2)
    for d in GROUPS:
        landed(d, 3)
    input_products(3)
    core_sum_send(3)
    column_sum_send(2)
    hidden_spread(0, 2)
    column_sum_send(3)
    row_sum_send(0)
    hidden_spread(1, 3)
    row_sum_send(1)
    hidden_spread(0, 3)
    row_sum_send(2)
    row_sum_send(3)
    weight_products(1)
    weight_products(0)
    hidden_landed(0, 3)
    hidden_landed(1, 3)
    out(back.at[HIDDEN], hidden_out, 2)
    row_sum_finish()
    peak_ref[0] = jnp.max(pk[3, 0:1])
    peak_ref[1] = jnp.max(pk[3, 1:2])
    column_sum_sent()
    row_sum_sent()
    for copy in outs:
        copy.wait()
    for copy in sends:
        copy.wait_send()


def weight_kernel(gate_in, up_in, hidden, out_grad, ig_in, peak_in, gate_ref, up_ref, down_ref, ig_ref, peak_ref, down, sem):
    copies = []

    def store(src, dst):
        copy = pltpu.make_async_copy(src, dst, sem.at[len(copies)])
        copy.start()
        copies.append(copy)

    for k in range(0, gate_in.shape[0], 256):
        store(gate_in.at[k : k + 256], gate_ref.at[k : k + 256])
        store(up_in.at[k : k + 256], up_ref.at[k : k + 256])
    for k in range(0, down.shape[0], 128):
        down[k : k + 128] = dot_rows(hidden[:, k : k + 128], out_grad[...]).astype(jnp.bfloat16)
        store(down.at[k : k + 128], down_ref.at[k : k + 128])
    ig_ref[...] = ig_in[...]
    peak_ref[0] = peak_in[0]
    peak_ref[1] = peak_in[1]
    for copy in copies:
        copy.wait()


def local(tokens, gate_weight, up_weight, down_weight, out_grad):
    bf16, f32 = jnp.bfloat16, jnp.float32
    width, hid = gate_weight.shape
    group, size = 2 * NX * ROWS, NY * ROWS
    total = 2 * NX * size
    anywhere = pl.BlockSpec(memory_space=pl.ANY)
    vmem, dma = pltpu.VMEM, pltpu.SemaphoreType.DMA
    args = [pltpu.with_memory_space_constraint(v, pltpu.HBM) for v in (tokens, out_grad, gate_weight, up_weight, down_weight)]
    input_grad, peaks, gate_grad, up_grad, hidden, grad_all = pl.pallas_call(
        main_kernel,
        name="slab",
        out_shape=(
            jax.ShapeDtypeStruct((ROWS, width), bf16),
            jax.ShapeDtypeStruct((2,), f32),
            jax.ShapeDtypeStruct((width, hid), bf16),
            jax.ShapeDtypeStruct((width, hid), bf16),
            jax.ShapeDtypeStruct((2 * NX, size, hid), bf16),
            jax.ShapeDtypeStruct((2 * NX, size, width), bf16),
        ),
        in_specs=[pl.BlockSpec(memory_space=pltpu.HBM)] * 5,
        out_specs=(
            pl.BlockSpec(memory_space=pltpu.VMEM),
            pl.BlockSpec(memory_space=pltpu.SMEM),
            anywhere,
            anywhere,
            anywhere,
            anywhere,
        ),
        scratch_shapes=[
            vmem((2, 2 * NX, size, width), bf16),
            vmem((width, hid), bf16),
            vmem((width, hid), bf16),
            vmem((hid, width), bf16),
            vmem((width, hid), bf16),
            vmem((hid, width), bf16),
            vmem((hid, width), bf16),
            vmem((NY, 3, group, hid), f32),
            vmem((2, NY, 4, 3, ROWS, hid), bf16),
            vmem((2, NY, 4, 3, ROWS, hid), bf16),
            vmem((3, 2 * NX, size, hid), bf16),
            vmem((2, 2 * NX, size, hid), bf16),
            vmem((2, width, hid), bf16),
            vmem((2, 2, NZ * ROWS, width), bf16),
            vmem((2, NZ * ROWS, width), bf16),
            vmem((2, NZ * ROWS, width), bf16),
            vmem((2, NZ * ROWS, width), bf16),
            vmem((NZ * ROWS, width), bf16),
            vmem((8, ROWS, width), bf16),
            vmem((4, 2, 128), f32),
            vmem((17, 2, 128), f32),
            dma((5,)),
            dma((2, 3)), dma((2, 3)), dma((2, 4)), dma((2, 4)), dma((2, 3, 4)), dma((2, 3, 4)), dma((2, 3)), dma((2, 3)),
            dma((2, NY, 4, 2)), dma((2, NY, 4, 2)), dma((2, NY, 4)), dma((2, NY, 4)), dma((2, 2, 4)), dma((2, 2, 4)),
            dma((17,)), dma((17,)), dma((4,)), dma((4,)), dma((4, 2)), dma((4, 2)), dma((8,)), dma((8,)), dma((5,)),
        ],
        compiler_params=pltpu.CompilerParams(collective_id=0, has_side_effects=True, vmem_limit_bytes=40 * 2**20),
    )(*args)
    whole = pl.BlockSpec(memory_space=pltpu.VMEM)
    smem = pl.BlockSpec(memory_space=pltpu.SMEM)
    gate_grad, up_grad, down_grad, input_grad, peaks = pl.pallas_call(
        weight_kernel,
        name="weight_grads",
        out_shape=(
            jax.ShapeDtypeStruct((width, hid), bf16),
            jax.ShapeDtypeStruct((width, hid), bf16),
            jax.ShapeDtypeStruct((hid, width), bf16),
            jax.ShapeDtypeStruct((ROWS, width), bf16),
            jax.ShapeDtypeStruct((2,), f32),
        ),
        in_specs=[anywhere, anywhere, whole, whole, whole, smem],
        out_specs=(anywhere, anywhere, anywhere, whole, smem),
        scratch_shapes=[vmem((hid, width), bf16), dma((16,))],
        compiler_params=pltpu.CompilerParams(vmem_limit_bytes=16 * 2**20),
    )(gate_grad, up_grad, hidden.reshape(total, hid), grad_all.reshape(total, width), input_grad, peaks)
    return input_grad, gate_grad, up_grad, down_grad, peaks


def solution(mesh):
    in_specs = (P("gy", "gx"), P("gx", "gy"), P("gx", "gy"), P("gy", "gx"), P("gy", "gx"))
    out_specs = (P("gy", "gx"), P("gx", "gy"), P("gx", "gy"), P("gy", "gx"), P())
    return jax.shard_map(local, mesh=mesh, in_specs=in_specs, out_specs=out_specs, check_vma=False)
```

```python
import functools

import jax
import jax.numpy as jnp
from jax import lax
from jax.experimental import pallas as pl
from jax.experimental.pallas import tpu as pltpu
from jax.sharding import PartitionSpec as P

MESH = pl.DeviceIdType.MESH
FP8_MAX = 57344.0
HEADROOM = 8.0
TOP = HEADROOM * FP8_MAX
NZ, NY, NX, ROWS = 8, 4, 4, 16
GROUPS = (0, 1, 3, 2)
FIRST = 0
GATE, UP, HGRAD = 0, 1, 2
PRE_GATE, PRE_UP, HIDDEN = 0, 1, 2


def dot(a, b):
    return jnp.dot(a, b, preferred_element_type=jnp.float32)


def dot_rows(a, b):
    return lax.dot_general(a, b, (((0,), (0,)), ((), ())), preferred_element_type=jnp.float32)


def device(z, y, x, c):
    return (lax.rem(z + NZ, NZ), (lax.rem(y + NY, NY) * NX + lax.rem(x + NX, NX)) * 2 + c)


def main_kernel(
    tok_hbm, grad_hbm, wg_hbm, wu_hbm, wd_hbm,
    ig_ref, peak_ref, gate_out, up_out, hidden_out, grad_out,
    xy, wg, wu, wd, wdt, wgt, wut, part, rs_send, rs_recv, back, coded, w_grad, ig_part, ig_core, ig_sum, ig_recv, ig_last, row_sum, row_recv,
    pk, pk_recv,
    w_sem, x_send, x_recv, f_send, f_recv, y_send, y_recv, g_send, g_recv,
    r_send, r_recv, a_send, a_recv, h_send, h_recv, p_send, p_recv, b_send, b_recv, c_send, c_recv, l_send, l_recv, d_send, d_recv, o_sem,
):
    z, gy = lax.axis_index("gx"), lax.axis_index("gy")
    y, x, c = gy // 8, lax.rem(gy // 2, NX), lax.rem(gy, 2)
    mine = c * NX + x
    partner = device(z, y, x, 1 - c)
    ups = (device(z + 1, y, x, c), device(z - 1, y, x, c))
    sends, outs = [], []

    def remote(src, dst, s_sem, r_sem, dev):
        return pltpu.make_async_remote_copy(
            src_ref=src, dst_ref=dst, send_sem=s_sem, recv_sem=r_sem, device_id=dev, device_id_type=MESH
        )

    def send(src, dst, s_sem, r_sem, dev):
        copy = remote(src, dst, s_sem, r_sem, dev)
        copy.start()
        sends.append(copy)

    def arrived(ref, s_sem, r_sem):
        remote(ref, ref, s_sem, r_sem, partner).wait_recv()

    def rows(j, n=1):
        return pl.ds(pl.multiple_of(j * ROWS, ROWS), n * ROWS)

    def of(d, n=1):
        return slice(d * ROWS, (d + n) * ROWS)

    def chunk(k):
        return lax.rem(z + k + 2 * NZ, NZ)

    w_copies = [
        pltpu.make_async_copy(src, dst, w_sem.at[i])
        for i, (src, dst) in enumerate(
            ((tok_hbm, xy.at[0, mine, of(0)]), (grad_hbm, xy.at[1, mine, of(0)]), (wd_hbm, wd), (wg_hbm, wg), (wu_hbm, wu))
        )
    ]
    for copy in w_copies:
        copy.start()

    barrier = pltpu.get_barrier_semaphore()
    greet = [partner, *ups]
    greet += [device(z, y, x + i, c) for i in (1, 2, 3)] + [device(z, y + i, x, c) for i in (1, 2, 3)]
    for dev in greet:
        pl.semaphore_signal(barrier, inc=1, device_id=dev, device_id_type=MESH)
    w_copies[0].wait()
    w_copies[1].wait()
    pl.semaphore_wait(barrier, len(greet))

    def row_send(a):
        ref = xy.at[a, mine, of(0)]
        for i in (1, 3, 2):
            send(ref, ref, x_send.at[a, i - 1], x_recv.at[a, i - 1], device(z, y, x + i, c))
        send(ref, ref, f_send.at[a, 0], f_recv.at[a, 0], partner)

    def column_send(a, piece, dists):
        j = c * NX + lax.rem(x - piece + NX, NX)
        for i in dists:
            send(
                xy.at[a, j, of(0)], xy.at[a, j, of(4 - i)], y_send.at[a, i - 1, piece], y_recv.at[a, i - 1, piece],
                device(z, y + i, x, c),
            )

    def row_forward(a, i):
        ref = xy.at[a, c * NX + lax.rem(x - i + NX, NX), of(0)]
        arrived(ref, x_send.at[a, i - 1], x_recv.at[a, i - 1])
        send(ref, ref, f_send.at[a, i], f_recv.at[a, i], partner)
        column_send(a, i, (1, 3))

    def column_far(a):
        for piece in range(4):
            column_send(a, piece, (2,))

    def row_done(a):
        for i in range(4):
            ref = xy.at[a, (1 - c) * NX + lax.rem(x - i + NX, NX), of(0)]
            arrived(ref, f_send.at[a, i], f_recv.at[a, i])

    def half(a, d, core):
        return xy.at[a, pl.ds(core * NX, NX), of(d)]

    def column_forward(a, i):
        for piece in (0, 1, 3, 2):
            ref = xy.at[a, c * NX + lax.rem(x - piece + NX, NX), of(4 - i)]
            arrived(ref, y_send.at[a, i - 1, piece], y_recv.at[a, i - 1, piece])
        ref = half(a, 4 - i, c)
        send(ref, ref, g_send.at[a, i - 1], g_recv.at[a, i - 1], partner)

    def column_done(a, d):
        if d:
            arrived(half(a, d, 1 - c), g_send.at[a, 3 - d], g_recv.at[a, 3 - d])

    def group(a, d):
        return xy[a, :, of(d)].reshape(2 * NX * ROWS, xy.shape[3])

    def transpose_down():
        w_copies[2].wait()
        wdt[...] = wd[...].T

    def transpose_gate():
        wgt[...] = wg[...].T

    def transpose_up():
        wut[...] = wu[...].T

    def forward_products(d):
        if d == 0:
            w_copies[3].wait()
            w_copies[4].wait()
        column_done(0, d)
        part[d, GATE] = dot(group(0, d), wg[...])
        part[d, UP] = dot(group(0, d), wu[...])

    def grad_products(d):
        column_done(1, d)
        part[d, HGRAD] = dot(group(1, d), wdt[...])

    def span(kind, s, side, d):
        if kind == "gu":
            return (0, 2) if s else ((0, 1), (1, 2))[side]
        return (2, 3) if s or (side == 0) == (d in GROUPS[:2]) else None

    def reduce_step(kind, d, s):
        k = 0 if kind == "gu" else 1
        for side in (0, 1):
            now = span(kind, s, side, d)
            if now is None:
                continue
            j = chunk(4 - s if side == 0 else s - 4)
            before = span(kind, s - 1, side, d) if s else None
            if before is not None:
                lo, hi = before
                arrived(rs_recv.at[side, d, s - 1, lo:hi], r_send.at[side, d, s - 1, k], r_recv.at[side, d, s - 1, k])
            for a in range(*now):
                total = part[d, a, rows(j)]
                if before is not None and before[0] <= a < before[1]:
                    total += rs_recv[side, d, s - 1, a].astype(jnp.float32)
                rs_send[side, d, s, a] = total.astype(jnp.bfloat16)
            lo, hi = now
            send(
                rs_send.at[side, d, s, lo:hi], rs_recv.at[side, d, s, lo:hi],
                r_send.at[side, d, s, k], r_recv.at[side, d, s, k], ups[side],
            )

    def finish(d):
        for side in (0, 1):
            arrived(rs_recv.at[side, d, 3, 0:2], r_send.at[side, d, 3, 0], r_recv.at[side, d, 3, 0])
            arrived(rs_recv.at[side, d, 3, 2:3], r_send.at[side, d, 3, 1], r_recv.at[side, d, 3, 1])
        total = [
            part[d, a, rows(z)] + rs_recv[0, d, 3, a].astype(jnp.float32) + rs_recv[1, d, 3, a].astype(jnp.float32)
            for a in range(3)
        ]
        gate, up_val, hidden_grad = total
        sigma = jax.nn.sigmoid(gate)
        act = gate * sigma
        slope = sigma * (1.0 + gate * (1.0 - sigma))
        pre_gate = hidden_grad * up_val * slope
        pre_up = hidden_grad * act
        back[PRE_GATE, z, of(d)] = pre_gate.astype(jnp.bfloat16)
        back[PRE_UP, z, of(d)] = pre_up.astype(jnp.bfloat16)
        back[HIDDEN, z, of(d)] = (act * up_val).astype(jnp.bfloat16)
        for i, values in enumerate((pre_gate, pre_up)):
            top = jnp.abs(values)
            top = jnp.max(top.reshape(2, 8, top.shape[1]), axis=0)
            best = top[:, 0:128]
            for k in range(1, top.shape[1] // 128):
                best = jnp.maximum(best, top[:, k * 128 : (k + 1) * 128])
            best = jnp.max(best, axis=0, keepdims=True)
            if d != FIRST:
                best = jnp.maximum(best, pk[0, i : i + 1])
            pk[0, i : i + 1] = best

    def spread_ref(d, t, side):
        j = chunk(-t if side == 0 else t)
        lo, hi = (0, 2) if t < 3 else (side, side + 1)
        return back.at[lo:hi, j, of(d)]

    def landed(d, t):
        for side in (0, 1):
            j = chunk(-t - 1 if side == 0 else t + 1)
            lo, hi = (0, 2) if t < 3 else (side, side + 1)
            arrived(back.at[lo:hi, j, of(d)], a_send.at[side, d, t], a_recv.at[side, d, t])

    def spread(d, t):
        if t:
            landed(d, t - 1)
        for side in (0, 1):
            ref = spread_ref(d, t, side)
            send(ref, ref, a_send.at[side, d, t], a_recv.at[side, d, t], ups[side])

    def hidden_landed(part_of, t):
        for side in (0, 1):
            if t == 3 and side != part_of:
                continue
            j = chunk(-t - 1 if side == 0 else t + 1)
            arrived(back.at[HIDDEN, j, of(2 * part_of, 2)], h_send.at[side, part_of, t], h_recv.at[side, part_of, t])

    def hidden_spread(part_of, t):
        if t:
            hidden_landed(part_of, t - 1)
        for side in (0, 1):
            if t == 3 and side != part_of:
                continue
            ref = back.at[HIDDEN, chunk(-t if side == 0 else t), of(2 * part_of, 2)]
            send(ref, ref, h_send.at[side, part_of, t], h_recv.at[side, part_of, t], ups[side])

    row_devs = [device(z, y, x + i % 4, c if i < 4 else 1 - c) for i in range(1, 8)]
    col_devs = [device(z, y + i, x, c) for i in range(1, 4)]
    z_devs = [device(z + i, y, x, c) for i in range(1, 8)]
    stages = ((0, row_devs), (7, col_devs), (10, z_devs))

    def peaks_send(stage):
        first, devs = stages[stage]
        for i, dev in enumerate(devs):
            send(pk.at[stage], pk_recv.at[first + i], p_send.at[first + i], p_recv.at[first + i], dev)

    def peaks_wait(stage):
        first, devs = stages[stage]
        best = pk[stage]
        for i in range(len(devs)):
            arrived(pk_recv.at[first + i], p_send.at[first + i], p_recv.at[first + i])
        for i in range(len(devs)):
            best = jnp.maximum(best, pk_recv[first + i])
        pk[stage + 1] = best

    def safe_peaks():
        return jnp.max(pk[3, 0:1]) + 1e-6, jnp.max(pk[3, 1:2]) + 1e-6

    parts = ((0, 1, -1), (2, -2), (3, -3), (4,))
    starts = (0, 3, 5, 7)

    def input_products(q):
        peaks = safe_peaks()
        size = 4 * ROWS
        for i, which in enumerate((PRE_GATE, PRE_UP)):
            scale = TOP / peaks[i]
            for k in parts[q]:
                j = chunk(k)
                values = back[which, j].astype(jnp.float32) * scale
                coded[i, j] = jnp.clip(values, -FP8_MAX, FP8_MAX).astype(jnp.bfloat16)
        first, second = (
            dot(jnp.concatenate([coded[i, chunk(k)] for k in parts[q]], axis=0), w[...]) for i, w in enumerate((wgt, wut))
        )
        total = ((peaks[0] / TOP) * first + (peaks[1] / TOP) * second).astype(jnp.bfloat16)
        for m in range(len(parts[q])):
            for d in range(4):
                ig_part[d // 2, d % 2, of(starts[q] + m)] = total[m * size + d * ROWS : m * size + (d + 1) * ROWS]

    def last_sum_send():
        at = of(starts[3], len(parts[3]))
        for d in (2, 1, 3):
            send(ig_part.at[d // 2, d % 2, at], ig_last.at[d - 1], l_send.at[d - 1], l_recv.at[d - 1], device(z, y + d, x, c))

    def core_sum_send(q):
        at = of(starts[q], len(parts[q]))
        send(ig_part.at[:, 1 - c, at], ig_core.at[:, at], b_send.at[q], b_recv.at[q], partner)

    def column_copy(q, i):
        at = of(starts[q], len(parts[q]))
        dev = device(z, y + 2 * i + c, x, c)
        return remote(ig_sum.at[i, at], ig_recv.at[i, at], c_send.at[q, i], c_recv.at[q, i], dev)

    def column_sum_send(q):
        at = of(starts[q], len(parts[q]))
        arrived(ig_core.at[:, at], b_send.at[q], b_recv.at[q])
        for i in (1, 0):
            total = ig_part[i, c, at].astype(jnp.float32) + ig_core[i, at].astype(jnp.float32)
            ig_sum[i, at] = total.astype(jnp.bfloat16)
            copy = column_copy(q, i)
            if i:
                copy.start()
                continue

            @pl.when(c == 1)
            def _():
                copy.start()

            @pl.when(c == 0)
            def _():
                ig_recv[0, at] = ig_sum[0, at]

    def column_sum_sent():
        for q in range(3):
            column_copy(q, 1).wait_send()

            @pl.when(c == 1)
            def _():
                column_copy(q, 0).wait_send()

    def row_copy(q, m):
        j = chunk(parts[q][m])
        ref = row_sum.at[of(starts[q] + m)]
        k = starts[q] + m
        return j, ref, remote(ref, row_recv.at[mine], d_send.at[k], d_recv.at[mine], device(z, y, lax.rem(j, NX), j // NX))

    def row_sum_send(q):
        at = of(starts[q], len(parts[q]))
        if q == 3:
            total = ig_part[0, 0, at].astype(jnp.float32)
            for d in (1, 3, 2):
                arrived(ig_last.at[d - 1], l_send.at[d - 1], l_recv.at[d - 1])
                total += ig_last[d - 1].astype(jnp.float32)
        else:
            arrived(ig_recv.at[1, at], c_send.at[q, 1], c_recv.at[q, 1])

            @pl.when(c == 1)
            def _():
                arrived(ig_recv.at[0, at], c_send.at[q, 0], c_recv.at[q, 0])

            total = ig_recv[0, at].astype(jnp.float32) + ig_recv[1, at].astype(jnp.float32)
        row_sum[at] = total.astype(jnp.bfloat16)
        for m in range(len(parts[q])):
            j, ref, copy = row_copy(q, m)

            @pl.when(j != mine)
            def _():
                copy.start()

            @pl.when(j == mine)
            def _():
                row_recv[mine] = ref[...]

    def row_sum_finish():
        for i in range(1, 8):
            src = lax.rem(mine + i, 8)
            arrived(row_recv.at[src], d_send.at[0], d_recv.at[src])
        total = row_recv[0].astype(jnp.float32)
        for i in range(1, 8):
            total += row_recv[i].astype(jnp.float32)
        ig_ref[...] = total.astype(jnp.bfloat16)

    def row_sum_sent():
        for q in range(4):
            for m in range(len(parts[q])):
                j, _, copy = row_copy(q, m)

                @pl.when(j != mine)
                def _():
                    copy.wait_send()

    def weight_products(i):
        scale = safe_peaks()[i] / TOP
        width = xy.shape[3]
        total = 2 * NX * 4 * ROWS
        right = coded[i].reshape(total, coded.shape[3])
        for k in range(0, width, 256):
            left = xy[0, :, :, k : k + 256].reshape(total, 256)
            w_grad[i, k : k + 256] = (scale * dot_rows(left, right)).astype(jnp.bfloat16)
        copy = pltpu.make_async_copy(w_grad.at[i], (gate_out, up_out)[i], o_sem.at[i])
        copy.start()
        outs.append(copy)

    def out(src, dst, sem):
        copy = pltpu.make_async_copy(src, dst, o_sem.at[sem])
        copy.start()
        outs.append(copy)

    row_send(0)
    transpose_down()
    row_send(1)
    column_send(0, 0, (1, 3))
    column_send(1, 0, (1, 3))
    row_forward(0, 3)
    row_forward(0, 1)
    row_forward(0, 2)
    column_far(0)
    row_forward(1, 1)
    row_forward(1, 3)
    row_done(0)
    forward_products(0)
    row_forward(1, 2)
    reduce_step("gu", 0, 0)
    column_forward(0, 3)
    column_far(1)
    column_forward(0, 1)
    row_done(1)
    grad_products(0)
    reduce_step("hg", 0, 0)
    forward_products(1)
    reduce_step("gu", 1, 0)
    reduce_step("gu", 0, 1)
    forward_products(3)
    reduce_step("hg", 0, 1)
    column_forward(1, 1)
    reduce_step("gu", 3, 0)
    reduce_step("gu", 1, 1)
    column_forward(1, 3)
    column_forward(0, 2)
    grad_products(3)
    reduce_step("hg", 3, 0)
    reduce_step("gu", 0, 2)
    grad_products(1)
    reduce_step("hg", 0, 2)
    column_forward(1, 2)
    reduce_step("gu", 3, 1)
    reduce_step("hg", 1, 0)
    forward_products(2)
    reduce_step("gu", 1, 2)
    grad_products(2)
    out(xy.at[1], grad_out, 3)
    reduce_step("gu", 0, 3)
    reduce_step("gu", 2, 0)
    reduce_step("hg", 2, 0)
    reduce_step("hg", 0, 3)
    reduce_step("hg", 1, 1)
    transpose_up()
    reduce_step("hg", 3, 1)
    reduce_step("gu", 3, 2)
    reduce_step("gu", 2, 1)
    reduce_step("hg", 2, 1)
    finish(0)
    reduce_step("hg", 1, 2)
    reduce_step("gu", 1, 3)
    reduce_step("hg", 3, 2)
    reduce_step("gu", 2, 2)
    reduce_step("hg", 2, 2)
    reduce_step("hg", 1, 3)
    reduce_step("gu", 3, 3)
    reduce_step("hg", 3, 3)
    reduce_step("gu", 2, 3)
    reduce_step("hg", 2, 3)
    spread(0, 0)
    finish(1)
    finish(3)
    spread(3, 0)
    spread(1, 0)
    finish(2)
    peaks_send(0)
    spread(2, 0)
    spread(0, 1)
    hidden_spread(0, 0)
    spread(1, 1)
    transpose_gate()
    spread(3, 1)
    peaks_wait(0)
    peaks_send(1)
    spread(2, 1)
    peaks_wait(1)
    peaks_send(2)
    spread(0, 2)
    spread(3, 2)
    spread(1, 2)
    spread(2, 2)
    hidden_spread(1, 0)
    hidden_spread(0, 1)
    spread(0, 3)
    peaks_wait(2)
    input_products(0)
    core_sum_send(0)
    spread(3, 3)
    input_products(1)
    column_sum_send(0)
    core_sum_send(1)
    spread(1, 3)
    spread(2, 3)
    hidden_spread(1, 1)
    input_products(2)
    core_sum_send(2)
    column_sum_send(1)
    hidden_spread(0, 2)
    column_sum_send(2)
    for d in GROUPS:
        landed(d, 3)
    input_products(3)
    hidden_spread(1, 2)
    last_sum_send()
    row_sum_send(0)
    row_sum_send(1)
    hidden_spread(0, 3)
    row_sum_send(2)
    hidden_spread(1, 3)
    row_sum_send(3)
    weight_products(1)
    weight_products(0)
    hidden_landed(0, 3)
    hidden_landed(1, 3)
    out(back.at[HIDDEN], hidden_out, 2)
    row_sum_finish()
    peak_ref[0] = jnp.max(pk[3, 0:1])
    peak_ref[1] = jnp.max(pk[3, 1:2])
    column_sum_sent()
    row_sum_sent()
    for copy in outs:
        copy.wait()
    for copy in sends:
        copy.wait_send()


def weight_kernel(gate_in, up_in, hidden, out_grad, ig_in, peak_in, gate_ref, up_ref, down_ref, ig_ref, peak_ref, down, sem):
    copies = []

    def store(src, dst):
        copy = pltpu.make_async_copy(src, dst, sem.at[len(copies)])
        copy.start()
        copies.append(copy)

    for k in range(0, gate_in.shape[0], 256):
        store(gate_in.at[k : k + 256], gate_ref.at[k : k + 256])
        store(up_in.at[k : k + 256], up_ref.at[k : k + 256])
    for k in range(0, down.shape[0], 128):
        down[k : k + 128] = dot_rows(hidden[:, k : k + 128], out_grad[...]).astype(jnp.bfloat16)
        store(down.at[k : k + 128], down_ref.at[k : k + 128])
    ig_ref[...] = ig_in[...]
    peak_ref[0] = peak_in[0]
    peak_ref[1] = peak_in[1]
    for copy in copies:
        copy.wait()


def local(tokens, gate_weight, up_weight, down_weight, out_grad):
    bf16, f32 = jnp.bfloat16, jnp.float32
    width, hid = gate_weight.shape
    group, size = 2 * NX * ROWS, NY * ROWS
    total = 2 * NX * size
    anywhere = pl.BlockSpec(memory_space=pl.ANY)
    vmem, dma = pltpu.VMEM, pltpu.SemaphoreType.DMA
    args = [pltpu.with_memory_space_constraint(v, pltpu.HBM) for v in (tokens, out_grad, gate_weight, up_weight, down_weight)]
    input_grad, peaks, gate_grad, up_grad, hidden, grad_all = pl.pallas_call(
        main_kernel,
        name="slab",
        out_shape=(
            jax.ShapeDtypeStruct((ROWS, width), bf16),
            jax.ShapeDtypeStruct((2,), f32),
            jax.ShapeDtypeStruct((width, hid), bf16),
            jax.ShapeDtypeStruct((width, hid), bf16),
            jax.ShapeDtypeStruct((2 * NX, size, hid), bf16),
            jax.ShapeDtypeStruct((2 * NX, size, width), bf16),
        ),
        in_specs=[pl.BlockSpec(memory_space=pltpu.HBM)] * 5,
        out_specs=(
            pl.BlockSpec(memory_space=pltpu.VMEM),
            pl.BlockSpec(memory_space=pltpu.SMEM),
            anywhere,
            anywhere,
            anywhere,
            anywhere,
        ),
        scratch_shapes=[
            vmem((2, 2 * NX, size, width), bf16),
            vmem((width, hid), bf16),
            vmem((width, hid), bf16),
            vmem((hid, width), bf16),
            vmem((width, hid), bf16),
            vmem((hid, width), bf16),
            vmem((hid, width), bf16),
            vmem((NY, 3, group, hid), f32),
            vmem((2, NY, 4, 3, ROWS, hid), bf16),
            vmem((2, NY, 4, 3, ROWS, hid), bf16),
            vmem((3, 2 * NX, size, hid), bf16),
            vmem((2, 2 * NX, size, hid), bf16),
            vmem((2, width, hid), bf16),
            vmem((2, 2, NZ * ROWS, width), bf16),
            vmem((2, NZ * ROWS, width), bf16),
            vmem((2, NZ * ROWS, width), bf16),
            vmem((2, NZ * ROWS, width), bf16),
            vmem((3, ROWS, width), bf16),
            vmem((NZ * ROWS, width), bf16),
            vmem((8, ROWS, width), bf16),
            vmem((4, 2, 128), f32),
            vmem((17, 2, 128), f32),
            dma((5,)),
            dma((2, 3)), dma((2, 3)), dma((2, 4)), dma((2, 4)), dma((2, 3, 4)), dma((2, 3, 4)), dma((2, 3)), dma((2, 3)),
            dma((2, NY, 4, 2)), dma((2, NY, 4, 2)), dma((2, NY, 4)), dma((2, NY, 4)), dma((2, 2, 4)), dma((2, 2, 4)),
            dma((17,)), dma((17,)), dma((3,)), dma((3,)), dma((3, 2)), dma((3, 2)), dma((3,)), dma((3,)), dma((8,)), dma((8,)), dma((5,)),
        ],
        compiler_params=pltpu.CompilerParams(collective_id=0, has_side_effects=True, vmem_limit_bytes=40 * 2**20),
    )(*args)
    whole = pl.BlockSpec(memory_space=pltpu.VMEM)
    smem = pl.BlockSpec(memory_space=pltpu.SMEM)
    gate_grad, up_grad, down_grad, input_grad, peaks = pl.pallas_call(
        weight_kernel,
        name="weight_grads",
        out_shape=(
            jax.ShapeDtypeStruct((width, hid), bf16),
            jax.ShapeDtypeStruct((width, hid), bf16),
            jax.ShapeDtypeStruct((hid, width), bf16),
            jax.ShapeDtypeStruct((ROWS, width), bf16),
            jax.ShapeDtypeStruct((2,), f32),
        ),
        in_specs=[anywhere, anywhere, whole, whole, whole, smem],
        out_specs=(anywhere, anywhere, anywhere, whole, smem),
        scratch_shapes=[vmem((hid, width), bf16), dma((16,))],
        compiler_params=pltpu.CompilerParams(vmem_limit_bytes=16 * 2**20),
    )(gate_grad, up_grad, hidden.reshape(total, hid), grad_all.reshape(total, width), input_grad, peaks)
    return input_grad, gate_grad, up_grad, down_grad, peaks


def solution(mesh):
    in_specs = (P("gy", "gx"), P("gx", "gy"), P("gx", "gy"), P("gy", "gx"), P("gy", "gx"))
    out_specs = (P("gy", "gx"), P("gx", "gy"), P("gx", "gy"), P("gy", "gx"), P())
    return jax.shard_map(local, mesh=mesh, in_specs=in_specs, out_specs=out_specs, check_vma=False)
```

```python
import functools

import jax
import jax.numpy as jnp
from jax import lax
from jax.experimental import pallas as pl
from jax.experimental.pallas import tpu as pltpu
from jax.sharding import PartitionSpec as P

MESH = pl.DeviceIdType.MESH
FP8_MAX = 57344.0
HEADROOM = 8.0
TOP = HEADROOM * FP8_MAX
NZ, NY, NX, ROWS = 8, 4, 4, 16
GROUPS = (0, 1, 3, 2)
FIRST = 0
GATE, UP, HGRAD = 0, 1, 2
PRE_GATE, PRE_UP, HIDDEN = 0, 1, 2


def dot(a, b):
    return jnp.dot(a, b, preferred_element_type=jnp.float32)


def dot_rows(a, b):
    return lax.dot_general(a, b, (((0,), (0,)), ((), ())), preferred_element_type=jnp.float32)


def device(z, y, x, c):
    return (lax.rem(z + NZ, NZ), (lax.rem(y + NY, NY) * NX + lax.rem(x + NX, NX)) * 2 + c)


def main_kernel(
    tok_hbm, grad_hbm, wg_hbm, wu_hbm, wd_hbm,
    ig_ref, peak_ref, gate_out, up_out, hidden_out, grad_out,
    xy, wg, wu, wd, wdt, wgt, wut, part, rs_send, rs_recv, back, coded, w_grad, ig_part, ig_core, ig_sum, ig_recv, ig_last, row_sum, row_recv,
    pk, pk_recv,
    w_sem, x_send, x_recv, f_send, f_recv, y_send, y_recv, g_send, g_recv,
    r_send, r_recv, a_send, a_recv, h_send, h_recv, p_send, p_recv, b_send, b_recv, c_send, c_recv, l_send, l_recv, d_send, d_recv, o_sem,
):
    z, gy = lax.axis_index("gx"), lax.axis_index("gy")
    y, x, c = gy // 8, lax.rem(gy // 2, NX), lax.rem(gy, 2)
    mine = c * NX + x
    partner = device(z, y, x, 1 - c)
    ups = (device(z + 1, y, x, c), device(z - 1, y, x, c))
    sends, outs = [], []

    def remote(src, dst, s_sem, r_sem, dev):
        return pltpu.make_async_remote_copy(
            src_ref=src, dst_ref=dst, send_sem=s_sem, recv_sem=r_sem, device_id=dev, device_id_type=MESH
        )

    def send(src, dst, s_sem, r_sem, dev):
        copy = remote(src, dst, s_sem, r_sem, dev)
        copy.start()
        sends.append(copy)

    def arrived(ref, s_sem, r_sem):
        remote(ref, ref, s_sem, r_sem, partner).wait_recv()

    def rows(j, n=1):
        return pl.ds(pl.multiple_of(j * ROWS, ROWS), n * ROWS)

    def of(d, n=1):
        return slice(d * ROWS, (d + n) * ROWS)

    def chunk(k):
        return lax.rem(z + k + 2 * NZ, NZ)

    w_copies = [
        pltpu.make_async_copy(src, dst, w_sem.at[i])
        for i, (src, dst) in enumerate(
            ((tok_hbm, xy.at[0, mine, of(0)]), (grad_hbm, xy.at[1, mine, of(0)]), (wd_hbm, wd), (wg_hbm, wg), (wu_hbm, wu))
        )
    ]
    for copy in w_copies:
        copy.start()

    barrier = pltpu.get_barrier_semaphore()
    greet = [partner, *ups]
    greet += [device(z, y, x + i, c) for i in (1, 2, 3)] + [device(z, y + i, x, c) for i in (1, 2, 3)]
    for dev in greet:
        pl.semaphore_signal(barrier, inc=1, device_id=dev, device_id_type=MESH)
    w_copies[0].wait()
    w_copies[1].wait()
    pl.semaphore_wait(barrier, len(greet))

    def row_send(a):
        ref = xy.at[a, mine, of(0)]
        for i in (1, 3, 2):
            send(ref, ref, x_send.at[a, i - 1], x_recv.at[a, i - 1], device(z, y, x + i, c))
        send(ref, ref, f_send.at[a, 0], f_recv.at[a, 0], partner)

    def column_send(a, piece, dists):
        j = c * NX + lax.rem(x - piece + NX, NX)
        for i in dists:
            send(
                xy.at[a, j, of(0)], xy.at[a, j, of(4 - i)], y_send.at[a, i - 1, piece], y_recv.at[a, i - 1, piece],
                device(z, y + i, x, c),
            )

    def row_forward(a, i):
        ref = xy.at[a, c * NX + lax.rem(x - i + NX, NX), of(0)]
        arrived(ref, x_send.at[a, i - 1], x_recv.at[a, i - 1])
        send(ref, ref, f_send.at[a, i], f_recv.at[a, i], partner)
        column_send(a, i, (1, 3))

    def column_far(a):
        for piece in range(4):
            column_send(a, piece, (2,))

    def row_done(a):
        for i in range(4):
            ref = xy.at[a, (1 - c) * NX + lax.rem(x - i + NX, NX), of(0)]
            arrived(ref, f_send.at[a, i], f_recv.at[a, i])

    def half(a, d, core):
        return xy.at[a, pl.ds(core * NX, NX), of(d)]

    def column_forward(a, i):
        for piece in (0, 1, 3, 2):
            ref = xy.at[a, c * NX + lax.rem(x - piece + NX, NX), of(4 - i)]
            arrived(ref, y_send.at[a, i - 1, piece], y_recv.at[a, i - 1, piece])
        ref = half(a, 4 - i, c)
        send(ref, ref, g_send.at[a, i - 1], g_recv.at[a, i - 1], partner)

    def column_done(a, d):
        if d:
            arrived(half(a, d, 1 - c), g_send.at[a, 3 - d], g_recv.at[a, 3 - d])

    def group(a, d):
        return xy[a, :, of(d)].reshape(2 * NX * ROWS, xy.shape[3])

    def transpose_down():
        w_copies[2].wait()
        wdt[...] = wd[...].T

    def transpose_gate():
        wgt[...] = wg[...].T

    def transpose_up():
        wut[...] = wu[...].T

    def forward_products(d):
        if d == 0:
            w_copies[3].wait()
            w_copies[4].wait()
        column_done(0, d)
        part[d, GATE] = dot(group(0, d), wg[...])
        part[d, UP] = dot(group(0, d), wu[...])

    def grad_products(d):
        column_done(1, d)
        part[d, HGRAD] = dot(group(1, d), wdt[...])

    def span(kind, s, side, d):
        if kind == "gu":
            return (0, 2) if s else ((0, 1), (1, 2))[side]
        return (2, 3) if s or (side == 0) == (d in GROUPS[:2]) else None

    def reduce_step(kind, d, s):
        k = 0 if kind == "gu" else 1
        for side in (0, 1):
            now = span(kind, s, side, d)
            if now is None:
                continue
            j = chunk(4 - s if side == 0 else s - 4)
            before = span(kind, s - 1, side, d) if s else None
            if before is not None:
                lo, hi = before
                arrived(rs_recv.at[side, d, s - 1, lo:hi], r_send.at[side, d, s - 1, k], r_recv.at[side, d, s - 1, k])
            for a in range(*now):
                total = part[d, a, rows(j)]
                if before is not None and before[0] <= a < before[1]:
                    total += rs_recv[side, d, s - 1, a].astype(jnp.float32)
                rs_send[side, d, s, a] = total.astype(jnp.bfloat16)
            lo, hi = now
            send(
                rs_send.at[side, d, s, lo:hi], rs_recv.at[side, d, s, lo:hi],
                r_send.at[side, d, s, k], r_recv.at[side, d, s, k], ups[side],
            )

    def finish(d):
        for side in (0, 1):
            arrived(rs_recv.at[side, d, 3, 0:2], r_send.at[side, d, 3, 0], r_recv.at[side, d, 3, 0])
            arrived(rs_recv.at[side, d, 3, 2:3], r_send.at[side, d, 3, 1], r_recv.at[side, d, 3, 1])
        total = [
            part[d, a, rows(z)] + rs_recv[0, d, 3, a].astype(jnp.float32) + rs_recv[1, d, 3, a].astype(jnp.float32)
            for a in range(3)
        ]
        gate, up_val, hidden_grad = total
        sigma = jax.nn.sigmoid(gate)
        act = gate * sigma
        slope = sigma * (1.0 + gate * (1.0 - sigma))
        pre_gate = hidden_grad * up_val * slope
        pre_up = hidden_grad * act
        back[PRE_GATE, z, of(d)] = pre_gate.astype(jnp.bfloat16)
        back[PRE_UP, z, of(d)] = pre_up.astype(jnp.bfloat16)
        back[HIDDEN, z, of(d)] = (act * up_val).astype(jnp.bfloat16)
        for i, values in enumerate((pre_gate, pre_up)):
            top = jnp.abs(values)
            top = jnp.max(top.reshape(2, 8, top.shape[1]), axis=0)
            best = top[:, 0:128]
            for k in range(1, top.shape[1] // 128):
                best = jnp.maximum(best, top[:, k * 128 : (k + 1) * 128])
            best = jnp.max(best, axis=0, keepdims=True)
            if d != FIRST:
                best = jnp.maximum(best, pk[0, i : i + 1])
            pk[0, i : i + 1] = best

    def spread_ref(d, t, side):
        j = chunk(-t if side == 0 else t)
        lo, hi = (0, 2) if t < 3 else (side, side + 1)
        return back.at[lo:hi, j, of(d)]

    def landed(d, t):
        for side in (0, 1):
            j = chunk(-t - 1 if side == 0 else t + 1)
            lo, hi = (0, 2) if t < 3 else (side, side + 1)
            arrived(back.at[lo:hi, j, of(d)], a_send.at[side, d, t], a_recv.at[side, d, t])

    def spread(d, t):
        if t:
            landed(d, t - 1)
        for side in (0, 1):
            ref = spread_ref(d, t, side)
            send(ref, ref, a_send.at[side, d, t], a_recv.at[side, d, t], ups[side])

    def hidden_landed(part_of, t):
        for side in (0, 1):
            if t == 3 and side != part_of:
                continue
            j = chunk(-t - 1 if side == 0 else t + 1)
            arrived(back.at[HIDDEN, j, of(2 * part_of, 2)], h_send.at[side, part_of, t], h_recv.at[side, part_of, t])

    def hidden_spread(part_of, t):
        if t:
            hidden_landed(part_of, t - 1)
        for side in (0, 1):
            if t == 3 and side != part_of:
                continue
            ref = back.at[HIDDEN, chunk(-t if side == 0 else t), of(2 * part_of, 2)]
            send(ref, ref, h_send.at[side, part_of, t], h_recv.at[side, part_of, t], ups[side])

    row_devs = [device(z, y, x + i % 4, c if i < 4 else 1 - c) for i in range(1, 8)]
    col_devs = [device(z, y + i, x, c) for i in range(1, 4)]
    z_devs = [device(z + i, y, x, c) for i in range(1, 8)]
    stages = ((0, row_devs), (7, col_devs), (10, z_devs))

    def peaks_send(stage):
        first, devs = stages[stage]
        for i, dev in enumerate(devs):
            send(pk.at[stage], pk_recv.at[first + i], p_send.at[first + i], p_recv.at[first + i], dev)

    def peaks_wait(stage):
        first, devs = stages[stage]
        best = pk[stage]
        for i in range(len(devs)):
            arrived(pk_recv.at[first + i], p_send.at[first + i], p_recv.at[first + i])
        for i in range(len(devs)):
            best = jnp.maximum(best, pk_recv[first + i])
        pk[stage + 1] = best

    def safe_peaks():
        return jnp.max(pk[3, 0:1]) + 1e-6, jnp.max(pk[3, 1:2]) + 1e-6

    parts = ((0, 1, -1), (2, -2), (3, -3), (4,))
    starts = (0, 3, 5, 7)

    def input_products(q):
        peaks = safe_peaks()
        size = 4 * ROWS
        for i, which in enumerate((PRE_GATE, PRE_UP)):
            scale = TOP / peaks[i]
            for k in parts[q]:
                j = chunk(k)
                values = back[which, j].astype(jnp.float32) * scale
                coded[i, j] = jnp.clip(values, -FP8_MAX, FP8_MAX).astype(jnp.bfloat16)
        first, second = (
            dot(jnp.concatenate([coded[i, chunk(k)] for k in parts[q]], axis=0), w[...]) for i, w in enumerate((wgt, wut))
        )
        total = ((peaks[0] / TOP) * first + (peaks[1] / TOP) * second).astype(jnp.bfloat16)
        for m in range(len(parts[q])):
            for d in range(4):
                ig_part[d // 2, d % 2, of(starts[q] + m)] = total[m * size + d * ROWS : m * size + (d + 1) * ROWS]

    def last_sum_send():
        at = of(starts[3], len(parts[3]))
        for d in (2, 1, 3):
            send(ig_part.at[d // 2, d % 2, at], ig_last.at[d - 1], l_send.at[d - 1], l_recv.at[d - 1], device(z, y + d, x, c))

    def core_sum_send(q):
        at = of(starts[q], len(parts[q]))
        send(ig_part.at[:, 1 - c, at], ig_core.at[:, at], b_send.at[q], b_recv.at[q], partner)

    def column_copy(q, i):
        at = of(starts[q], len(parts[q]))
        dev = device(z, y + 2 * i + c, x, c)
        return remote(ig_sum.at[i, at], ig_recv.at[i, at], c_send.at[q, i], c_recv.at[q, i], dev)

    def column_sum_send(q):
        at = of(starts[q], len(parts[q]))
        arrived(ig_core.at[:, at], b_send.at[q], b_recv.at[q])
        for i in (1, 0):
            total = ig_part[i, c, at].astype(jnp.float32) + ig_core[i, at].astype(jnp.float32)
            ig_sum[i, at] = total.astype(jnp.bfloat16)
            copy = column_copy(q, i)
            if i:
                copy.start()
                continue

            @pl.when(c == 1)
            def _():
                copy.start()

            @pl.when(c == 0)
            def _():
                ig_recv[0, at] = ig_sum[0, at]

    def column_sum_sent():
        for q in range(3):
            column_copy(q, 1).wait_send()

            @pl.when(c == 1)
            def _():
                column_copy(q, 0).wait_send()

    def row_copy(q, m):
        j = chunk(parts[q][m])
        ref = row_sum.at[of(starts[q] + m)]
        k = starts[q] + m
        return j, ref, remote(ref, row_recv.at[mine], d_send.at[k], d_recv.at[mine], device(z, y, lax.rem(j, NX), j // NX))

    def row_sum_send(q):
        at = of(starts[q], len(parts[q]))
        if q == 3:
            total = ig_part[0, 0, at].astype(jnp.float32)
            for d in (1, 3, 2):
                arrived(ig_last.at[d - 1], l_send.at[d - 1], l_recv.at[d - 1])
                total += ig_last[d - 1].astype(jnp.float32)
        else:
            arrived(ig_recv.at[1, at], c_send.at[q, 1], c_recv.at[q, 1])

            @pl.when(c == 1)
            def _():
                arrived(ig_recv.at[0, at], c_send.at[q, 0], c_recv.at[q, 0])

            total = ig_recv[0, at].astype(jnp.float32) + ig_recv[1, at].astype(jnp.float32)
        row_sum[at] = total.astype(jnp.bfloat16)
        for m in range(len(parts[q])):
            j, ref, copy = row_copy(q, m)

            @pl.when(j != mine)
            def _():
                copy.start()

            @pl.when(j == mine)
            def _():
                row_recv[mine] = ref[...]

    def row_sum_finish():
        for i in range(1, 8):
            src = lax.rem(mine + i, 8)
            arrived(row_recv.at[src], d_send.at[0], d_recv.at[src])
        total = row_recv[0].astype(jnp.float32)
        for i in range(1, 8):
            total += row_recv[i].astype(jnp.float32)
        ig_ref[...] = total.astype(jnp.bfloat16)

    def row_sum_sent():
        for q in range(4):
            for m in range(len(parts[q])):
                j, _, copy = row_copy(q, m)

                @pl.when(j != mine)
                def _():
                    copy.wait_send()

    def weight_products(i):
        scale = safe_peaks()[i] / TOP
        width = xy.shape[3]
        total = 2 * NX * 4 * ROWS
        right = coded[i].reshape(total, coded.shape[3])
        for k in range(0, width, 256):
            left = xy[0, :, :, k : k + 256].reshape(total, 256)
            w_grad[i, k : k + 256] = (scale * dot_rows(left, right)).astype(jnp.bfloat16)
        copy = pltpu.make_async_copy(w_grad.at[i], (gate_out, up_out)[i], o_sem.at[i])
        copy.start()
        outs.append(copy)

    def out(src, dst, sem):
        copy = pltpu.make_async_copy(src, dst, o_sem.at[sem])
        copy.start()
        outs.append(copy)

    def settle(keep):
        for copy in sends[: len(sends) - keep]:
            copy.wait_send()
        del sends[: len(sends) - keep]

    row_send(0)
    transpose_down()
    row_send(1)
    column_send(0, 0, (1, 3))
    column_send(1, 0, (1, 3))
    row_forward(0, 3)
    row_forward(0, 1)
    row_forward(0, 2)
    column_far(0)
    row_forward(1, 1)
    row_forward(1, 3)
    row_done(0)
    forward_products(0)
    row_forward(1, 2)
    reduce_step("gu", 0, 0)
    column_forward(0, 3)
    column_far(1)
    column_forward(0, 1)
    row_done(1)
    grad_products(0)
    reduce_step("hg", 0, 0)
    forward_products(1)
    reduce_step("gu", 1, 0)
    reduce_step("gu", 0, 1)
    forward_products(3)
    reduce_step("hg", 0, 1)
    column_forward(1, 1)
    reduce_step("gu", 3, 0)
    reduce_step("gu", 1, 1)
    column_forward(1, 3)
    column_forward(0, 2)
    grad_products(3)
    reduce_step("hg", 3, 0)
    reduce_step("gu", 0, 2)
    grad_products(1)
    reduce_step("hg", 0, 2)
    column_forward(1, 2)
    reduce_step("gu", 3, 1)
    reduce_step("hg", 1, 0)
    forward_products(2)
    reduce_step("gu", 1, 2)
    grad_products(2)
    out(xy.at[1], grad_out, 3)
    reduce_step("gu", 0, 3)
    reduce_step("gu", 2, 0)
    reduce_step("hg", 2, 0)
    reduce_step("hg", 0, 3)
    reduce_step("hg", 1, 1)
    transpose_up()
    reduce_step("hg", 3, 1)
    reduce_step("gu", 3, 2)
    reduce_step("gu", 2, 1)
    reduce_step("hg", 2, 1)
    finish(0)
    reduce_step("hg", 1, 2)
    reduce_step("gu", 1, 3)
    reduce_step("hg", 3, 2)
    reduce_step("gu", 2, 2)
    reduce_step("hg", 2, 2)
    reduce_step("hg", 1, 3)
    reduce_step("gu", 3, 3)
    reduce_step("hg", 3, 3)
    reduce_step("gu", 2, 3)
    reduce_step("hg", 2, 3)
    spread(0, 0)
    finish(1)
    finish(3)
    spread(3, 0)
    spread(1, 0)
    finish(2)
    peaks_send(0)
    spread(2, 0)
    spread(0, 1)
    hidden_spread(0, 0)
    spread(1, 1)
    transpose_gate()
    spread(3, 1)
    peaks_wait(0)
    peaks_send(1)
    spread(2, 1)
    peaks_wait(1)
    peaks_send(2)
    spread(0, 2)
    spread(3, 2)
    spread(1, 2)
    spread(2, 2)
    hidden_spread(1, 0)
    hidden_spread(0, 1)
    spread(0, 3)
    settle(16)
    peaks_wait(2)
    input_products(0)
    core_sum_send(0)
    spread(3, 3)
    input_products(1)
    column_sum_send(0)
    core_sum_send(1)
    spread(1, 3)
    spread(2, 3)
    hidden_spread(1, 1)
    input_products(2)
    core_sum_send(2)
    column_sum_send(1)
    hidden_spread(0, 2)
    column_sum_send(2)
    for d in GROUPS:
        landed(d, 3)
    input_products(3)
    hidden_spread(1, 2)
    last_sum_send()
    row_sum_send(0)
    settle(16)
    row_sum_send(1)
    hidden_spread(0, 3)
    row_sum_send(2)
    hidden_spread(1, 3)
    row_sum_send(3)
    weight_products(1)
    weight_products(0)
    hidden_landed(0, 3)
    hidden_landed(1, 3)
    out(back.at[HIDDEN], hidden_out, 2)
    row_sum_finish()
    peak_ref[0] = jnp.max(pk[3, 0:1])
    peak_ref[1] = jnp.max(pk[3, 1:2])
    column_sum_sent()
    row_sum_sent()
    for copy in outs:
        copy.wait()
    for copy in sends:
        copy.wait_send()


def weight_kernel(gate_in, up_in, hidden, out_grad, ig_in, peak_in, gate_ref, up_ref, down_ref, ig_ref, peak_ref, down, sem):
    copies = []

    def store(src, dst):
        copy = pltpu.make_async_copy(src, dst, sem.at[len(copies)])
        copy.start()
        copies.append(copy)

    for k in range(0, gate_in.shape[0], 256):
        store(gate_in.at[k : k + 256], gate_ref.at[k : k + 256])
        store(up_in.at[k : k + 256], up_ref.at[k : k + 256])
    for k in range(0, down.shape[0], 128):
        down[k : k + 128] = dot_rows(hidden[:, k : k + 128], out_grad[...]).astype(jnp.bfloat16)
        store(down.at[k : k + 128], down_ref.at[k : k + 128])
    ig_ref[...] = ig_in[...]
    peak_ref[0] = peak_in[0]
    peak_ref[1] = peak_in[1]
    for copy in copies:
        copy.wait()


def local(tokens, gate_weight, up_weight, down_weight, out_grad):
    bf16, f32 = jnp.bfloat16, jnp.float32
    width, hid = gate_weight.shape
    group, size = 2 * NX * ROWS, NY * ROWS
    total = 2 * NX * size
    anywhere = pl.BlockSpec(memory_space=pl.ANY)
    vmem, dma = pltpu.VMEM, pltpu.SemaphoreType.DMA
    args = [pltpu.with_memory_space_constraint(v, pltpu.HBM) for v in (tokens, out_grad, gate_weight, up_weight, down_weight)]
    input_grad, peaks, gate_grad, up_grad, hidden, grad_all = pl.pallas_call(
        main_kernel,
        name="slab",
        out_shape=(
            jax.ShapeDtypeStruct((ROWS, width), bf16),
            jax.ShapeDtypeStruct((2,), f32),
            jax.ShapeDtypeStruct((width, hid), bf16),
            jax.ShapeDtypeStruct((width, hid), bf16),
            jax.ShapeDtypeStruct((2 * NX, size, hid), bf16),
            jax.ShapeDtypeStruct((2 * NX, size, width), bf16),
        ),
        in_specs=[pl.BlockSpec(memory_space=pltpu.HBM)] * 5,
        out_specs=(
            pl.BlockSpec(memory_space=pltpu.VMEM),
            pl.BlockSpec(memory_space=pltpu.SMEM),
            anywhere,
            anywhere,
            anywhere,
            anywhere,
        ),
        scratch_shapes=[
            vmem((2, 2 * NX, size, width), bf16),
            vmem((width, hid), bf16),
            vmem((width, hid), bf16),
            vmem((hid, width), bf16),
            vmem((width, hid), bf16),
            vmem((hid, width), bf16),
            vmem((hid, width), bf16),
            vmem((NY, 3, group, hid), f32),
            vmem((2, NY, 4, 3, ROWS, hid), bf16),
            vmem((2, NY, 4, 3, ROWS, hid), bf16),
            vmem((3, 2 * NX, size, hid), bf16),
            vmem((2, 2 * NX, size, hid), bf16),
            vmem((2, width, hid), bf16),
            vmem((2, 2, NZ * ROWS, width), bf16),
            vmem((2, NZ * ROWS, width), bf16),
            vmem((2, NZ * ROWS, width), bf16),
            vmem((2, NZ * ROWS, width), bf16),
            vmem((3, ROWS, width), bf16),
            vmem((NZ * ROWS, width), bf16),
            vmem((8, ROWS, width), bf16),
            vmem((4, 2, 128), f32),
            vmem((17, 2, 128), f32),
            dma((5,)),
            dma((2, 3)), dma((2, 3)), dma((2, 4)), dma((2, 4)), dma((2, 3, 4)), dma((2, 3, 4)), dma((2, 3)), dma((2, 3)),
            dma((2, NY, 4, 2)), dma((2, NY, 4, 2)), dma((2, NY, 4)), dma((2, NY, 4)), dma((2, 2, 4)), dma((2, 2, 4)),
            dma((17,)), dma((17,)), dma((3,)), dma((3,)), dma((3, 2)), dma((3, 2)), dma((3,)), dma((3,)), dma((8,)), dma((8,)), dma((5,)),
        ],
        compiler_params=pltpu.CompilerParams(collective_id=0, has_side_effects=True, vmem_limit_bytes=40 * 2**20),
    )(*args)
    whole = pl.BlockSpec(memory_space=pltpu.VMEM)
    smem = pl.BlockSpec(memory_space=pltpu.SMEM)
    gate_grad, up_grad, down_grad, input_grad, peaks = pl.pallas_call(
        weight_kernel,
        name="weight_grads",
        out_shape=(
            jax.ShapeDtypeStruct((width, hid), bf16),
            jax.ShapeDtypeStruct((width, hid), bf16),
            jax.ShapeDtypeStruct((hid, width), bf16),
            jax.ShapeDtypeStruct((ROWS, width), bf16),
            jax.ShapeDtypeStruct((2,), f32),
        ),
        in_specs=[anywhere, anywhere, whole, whole, whole, smem],
        out_specs=(anywhere, anywhere, anywhere, whole, smem),
        scratch_shapes=[vmem((hid, width), bf16), dma((16,))],
        compiler_params=pltpu.CompilerParams(vmem_limit_bytes=16 * 2**20),
    )(gate_grad, up_grad, hidden.reshape(total, hid), grad_all.reshape(total, width), input_grad, peaks)
    return input_grad, gate_grad, up_grad, down_grad, peaks


def solution(mesh):
    in_specs = (P("gy", "gx"), P("gx", "gy"), P("gx", "gy"), P("gy", "gx"), P("gy", "gx"))
    out_specs = (P("gy", "gx"), P("gx", "gy"), P("gx", "gy"), P("gy", "gx"), P())
    return jax.shard_map(local, mesh=mesh, in_specs=in_specs, out_specs=out_specs, check_vma=False)
```
